256 devices in a mesh: ctx: 32 (over z_lo, x, y), head: 8 (over z_hi, core).
Axes of the slice: x: 4, y: 4, z: 8 (z_hi: 4, z_lo: 2; z = z_hi * 2 + z_lo), core: 2. Of those that a mesh axis runs over, the one named last changes fastest.
Arguments:
- teacher_queries: bfloat16 [2048, 73728], P('ctx', 'head'), may hold values from -42 to 42
- latent_keys: bfloat16 [4096, 576], P('ctx'), may hold values from -6 to 6
- index_queries: bfloat16 [2048, 8192], P('ctx', 'head'), may hold values from -18 to 18
- index_keys: bfloat16 [4096, 128], P('ctx'), may hold values from -6 to 6
- index_weights: bfloat16 [2048, 64], P('ctx', 'head'), may hold values from 0.019897461 to 0.29882812
- block_start: int32 [64], P('ctx'), may hold values from 2048 to 4064, as said below
Outputs:
- index_logits: float32 [2048, 4096], P('ctx', 'head')
- divergence: float32 [2048], P('ctx')
The draws below stay inside these ranges and needn't reach their ends.
Inputs may be any that keep to these rules, and one draw needn't show every extreme that they name: `block_start`: each is a multiple of 32 plus 4096 - 2048; the blocks cover the last 2048 context positions, each position once.
All inputs are finite; a program needn't handle non-finite values.
Results may differ from the reference program's by a relative error of at most 0.0003.
Values may be sent and summed in bfloat16 or wider, within the bound.
A program may use at most 64 MiB of HBM per device.

```python
import math
import jax
import jax.numpy as jnp
from jax import lax

LATENT = 512
ROPE = 64
TEACHER_HEADS = 128
INDEX_HEADS = 64
INDEX_DIM = 128
QB = 32
QUERIES = 2048
KEYS = 4096
NQB = 64


def latent_base(key):
    raw = jnp.clip(jax.random.normal(jax.random.fold_in(key, 101), (KEYS, LATENT + ROPE), jnp.float32), -6.0, 6.0)
    rows = jnp.arange(KEYS)
    twin = (rows % 64 == 1) & (rows < KEYS // 2)
    return jnp.where(twin[:, None], raw, raw)


def index_base(key):
    raw = jnp.clip(jax.random.normal(jax.random.fold_in(key, 202), (KEYS, INDEX_DIM), jnp.float32), -6.0, 6.0)
    rows = jnp.arange(KEYS)
    twin = (rows % 64 == 1) & (rows < KEYS // 2)
    return jnp.where(twin[:, None], raw, raw)


def draw_latent_keys(key, part):
    return latent_base(key).astype(jnp.bfloat16)


def draw_teacher_queries(key, part):
    key = jax.random.fold_in(key, 2)
    queries = jnp.clip(jax.random.normal(key, (QUERIES, TEACHER_HEADS * (LATENT + ROPE)), jnp.float32), -6.0, 6.0)
    return queries.astype(jnp.bfloat16)


def draw_index_keys(key, part):
    return index_base(key).astype(jnp.bfloat16)


def draw_index_queries(key, part):
    key = jax.random.fold_in(key, 4)
    queries = jnp.clip(jax.random.normal(key, (QUERIES, INDEX_HEADS * INDEX_DIM), jnp.float32), -6.0, 6.0)
    return queries.astype(jnp.bfloat16)


def draw_block_start(key, part):
    key = jax.random.fold_in(key, 5)
    order = jax.random.permutation(key, NQB)
    return (KEYS - QUERIES + QB * order).astype(jnp.int32)


def level_of(own_key, dims, cuts, smallest, top_value):
    factor_of, own = 1.0, jax.random.fold_in(own_key, 6)
    for dim, blocks in cuts:
        heights = jnp.exp(jax.random.uniform(jax.random.fold_in(own, dim), (blocks,), jnp.float32, smallest / len(cuts), top_value / len(cuts)))
        factor_of = factor_of * jnp.repeat(heights, dims[dim] // blocks).reshape([-1 if axis == dim else 1 for axis in range(len(dims))])
    return factor_of


def setup_inputs(seed: int = 0) -> dict:
    streams_of = jax.random.split(jax.random.key(seed), 7)
    return {
        "teacher_queries": draw_teacher_queries(jax.random.fold_in(streams_of[6], 71), 0),
        "latent_keys": draw_latent_keys(jax.random.fold_in(streams_of[6], 71), 0),
        "index_queries": draw_index_queries(jax.random.fold_in(streams_of[6], 71), 0),
        "index_keys": draw_index_keys(jax.random.fold_in(streams_of[6], 71), 0),
        "index_weights": jnp.clip(jnp.exp(math.log(0.29882812) - 2.7092764 * jax.random.uniform(streams_of[4], (QUERIES, INDEX_HEADS), jnp.float32) ** level_of(streams_of[4], (QUERIES, INDEX_HEADS), ((0, 32), (1, 8)), -0.2, 0.2)), 0.019897461, 0.29882812).astype(jnp.bfloat16),
        "block_start": draw_block_start(jax.random.fold_in(streams_of[6], 71), 0),
    }


SCALE = 192.0 ** -0.5
NEG = -1e30


def reference(teacher_queries, latent_keys, index_queries, index_keys, index_weights, block_start):
    rows = jnp.arange(QUERIES, dtype=jnp.int32)
    positions = block_start[rows // QB] + rows % QB
    visible = jnp.arange(KEYS, dtype=jnp.int32)[None, :] <= positions[:, None]
    width = LATENT + ROPE

    def teacher_head(total, head_id):
        query = lax.dynamic_slice_in_dim(teacher_queries, head_id * width, width, 1)
        score = jnp.dot(query, latent_keys.T, preferred_element_type=jnp.float32) * SCALE
        score = jnp.where(visible, score, NEG)
        peak = jnp.max(score, axis=1, keepdims=True)
        expo = jnp.where(visible, jnp.exp(score - peak), 0.0)
        return total + expo / jnp.sum(expo, axis=1, keepdims=True), None

    probs, _ = lax.scan(teacher_head, jnp.zeros((QUERIES, KEYS), jnp.float32), jnp.arange(TEACHER_HEADS, dtype=jnp.int32))
    probs = probs / TEACHER_HEADS

    def index_head(total, head_id):
        query = lax.dynamic_slice_in_dim(index_queries, head_id * INDEX_DIM, INDEX_DIM, 1)
        weight = lax.dynamic_slice_in_dim(index_weights, head_id, 1, 1).astype(jnp.float32)
        inner = jnp.dot(query, index_keys.T, preferred_element_type=jnp.float32)
        return total + weight * jax.nn.relu(inner), None

    logits, _ = lax.scan(index_head, jnp.zeros((QUERIES, KEYS), jnp.float32), jnp.arange(INDEX_HEADS, dtype=jnp.int32))
    logits = jnp.where(visible, logits * INDEX_DIM ** -0.5, 0.0)
    masked = jnp.where(visible, logits, NEG)
    peak = jnp.max(masked, axis=1)
    total = jnp.sum(jnp.where(visible, jnp.exp(masked - peak[:, None]), 0.0), axis=1)
    entropy = jnp.sum(probs * jnp.log(jnp.where(probs > 0, probs, 1.0)), axis=1)
    cross = jnp.sum(probs * logits, axis=1)
    divergence = entropy - cross + peak + jnp.log(total)
    return logits, divergence
```

```python
import functools

import jax
import jax.numpy as jnp
from jax import lax
from jax.experimental import pallas as pl
from jax.experimental.pallas import tpu as pltpu
from jax.sharding import PartitionSpec as P

MESH = pl.DeviceIdType.MESH
F32, BF16 = jnp.float32, jnp.bfloat16
TEACHER_HEADS = 128
LATENT, ROPE, WIDTH, IDIM = 512, 64, 576, 128
NEG = -1e30
EXP_SCALE = 192.0 ** (-0.5) * 1.4426950408889634
INDEX_SCALE = 128.0 ** (-0.5)
ORDER = (0, 1, 3, 2)
SCORE_ROWS = 512


def unrolled(n, by, body, carry):
    def several(i, carry):
        for u in range(by):
            carry = body(i * by + u, carry)
        return carry

    return lax.fori_loop(0, n // by, several, carry)


def kernel(
    tq_hbm, lk_ref, iq_ref, ik_ref, iw_ref, bs_ref,
    out_ref, div_ref,
    tq, q_rows, keys, kc, ki, kct, kit, expo, peaks, sums, wts,
    iq_send, iq_all, iw_send, iw_recv, iw_all, logits, lg_send, lg_all,
    p_mine, p_twin, p_twin_in, p_z, p_z_in, div_all,
    copy_sem, send_sem, twin_out, last_out, first_out, key_sem, iq_sem, iw_sem, lg_sem, twin_sem, z_sem, div_sem,
):
    ctx, head = lax.axis_index("ctx"), lax.axis_index("head")
    zl, x, y = ctx // 16, (ctx // 4) % 4, ctx % 4
    zh, core = head // 2, head % 2
    z = zh * 2 + zl
    pu, pv = x + core * (y - x), y + core * (x - y)
    twin = (ctx, zh * 2 + 1 - core)

    def ctx_of(par, u, v):
        u, v = lax.rem(u, 4), lax.rem(v, 4)
        return par * 16 + (u + core * (v - u)) * 4 + v + core * (u - v)

    def z_device(dz):
        zz = (z + dz + 8) % 8
        return ((zz % 2) * 16 + x * 4 + y, (zz // 2) * 2 + core)

    u_devs = {d: (ctx_of(zl, pu + d, pv), head) for d in (1, 3, 2)}
    v_devs = {d: (ctx_of(zl, pu, pv + d), head) for d in (1, 3, 2)}
    first_dev = z_device(2 * core - 1)
    last_dev = z_device(1 - 2 * core)
    mates = [(ctx, (head + r) % 8) for r in range(1, 8)]

    tq_copy = pltpu.make_async_copy(tq_hbm, tq, copy_sem)
    tq_copy.start()

    barrier = pltpu.get_barrier_semaphore()
    partners = list(u_devs.values()) + list(v_devs.values()) + [first_dev, last_dev] + mates
    for dev in partners:
        pl.semaphore_signal(barrier, inc=1, device_id=dev, device_id_type=MESH)

    lat = [lk_ref[128 * t:128 * t + 128, :].T for t in range(4)]
    rope = jnp.concatenate([lk_ref[512:576, :].astype(F32), jnp.zeros((64, 128), F32)], axis=0).T
    for g in range(4):
        a, b = g * 32, g * 32 + 16
        for t in range(4):
            keys[ctx, g, :, 128 * t:128 * t + 128] = lat[t][a:a + 16]
            keys[ctx, g, :, 640 + 128 * t:768 + 128 * t] = lat[t][b:b + 16]
        keys[ctx, g, :, 512:640] = ik_ref[a:a + 16, :]
        keys[ctx, g, :, 1152:1280] = ik_ref[b:b + 16, :]
        keys[ctx, g, :, 1280:1408] = (rope[a:a + 16] + pltpu.roll(rope[b:b + 16], 64, 1)).astype(BF16)

    iqf = iq_ref[...].astype(F32)
    for d in range(8):
        iq_send[d] = jnp.concatenate(
            [iqf[8 * d:8 * d + 8, 128 * j:128 * j + 128] for j in range(8)], axis=0
        ).astype(BF16)
    weights = jnp.concatenate([iw_ref[...].astype(F32), jnp.zeros((8, 64), F32)], axis=1)
    weights = jnp.concatenate([weights, jnp.zeros((120, 128), F32)], axis=0).T
    iw_send[...] = weights[0:64]

    pl.semaphore_wait(barrier, len(partners))

    sends = []

    def remote(src, dst, out_sem, in_sem, dev):
        return pltpu.make_async_remote_copy(
            src_ref=src, dst_ref=dst, send_sem=out_sem, recv_sem=in_sem,
            device_id=dev, device_id_type=MESH,
        )

    def send(src, dst, in_sem, dev):
        copy = remote(src, dst, send_sem.at[len(sends)], in_sem, dev)
        copy.start()
        sends.append(copy)

    def recv(dst, in_sem):
        remote(dst, dst, send_sem.at[0], in_sem, twin).wait_recv()

    def item(block, group, n):
        return keys.at[block, pl.ds(group, n)], key_sem.at[block, group]

    def send_item(it, devs):
        for dev in devs:
            send(it[0], it[0], it[1], dev)

    def to_twin_core(block, group, n):
        ref = keys.at[block, pl.ds(group, n)]
        return remote(ref, ref, twin_out.at[block, group], key_sem.at[block, group], twin)

    def to_last(block):
        ref = keys.at[block, pl.ds(g0, 1)]
        return remote(ref, ref, last_out.at[block], key_sem.at[block, g0], last_dev)

    def first_along_v(eu):
        block = at(other, eu, 0)
        ref = keys.at[block, pl.ds(g0 + 1, 1)]
        return [
            remote(ref, ref, first_out.at[eu, dv], key_sem.at[block, g0 + 1], v_devs[dv])
            for dv in (1, 3, 2)
        ]

    near = lambda devs: [devs[1], devs[3], devs[2]]
    g0 = 2 * core
    other = 1 - zl
    twin_half = 1 - core
    at = lambda par, du, dv: ctx_of(par, pu + du, pv + dv)

    send_item(item(ctx, g0, 2), [v_devs[1], v_devs[3], u_devs[1], u_devs[3], u_devs[2], v_devs[2]])
    send_item(item(ctx, g0 + 1, 1), [first_dev])
    to_last(ctx).start()
    for r, dev in enumerate(mates):
        d = (head + r + 1) % 8
        send(iq_send.at[d], iq_all.at[pl.ds(pl.multiple_of(head * 64, 64), 64)], iq_sem.at[head], dev)
        send(iw_send.at[pl.ds(pl.multiple_of(d * 8, 8), 8)], iw_recv.at[head], iw_sem.at[head], dev)

    tq_copy.wait()
    lane = lax.broadcasted_iota(jnp.int32, (64, 128), 1)

    def prepare(i, carry):
        base = pl.multiple_of(i * 1152, 128)
        row = pl.multiple_of(i * 128, 128)
        q_rows[pl.ds(row, 64), 0:512] = tq[:, pl.ds(base, 512)]
        tiles = [tq[:, pl.ds(base + 512 + 128 * t, 128)].astype(F32) for t in range(5)]
        q_rows[pl.ds(row, 64), 512:640] = jnp.where(lane < 64, tiles[0], 0.0).astype(BF16)
        rolled = [pltpu.roll(t, 64, 1) for t in tiles]
        rolled.append(jnp.zeros_like(rolled[0]))
        for t in range(5):
            q_rows[pl.ds(row + 64, 64), 128 * t:128 * t + 128] = jnp.where(
                lane < 64, rolled[t], rolled[t + 1]
            ).astype(BF16)
        return carry

    lax.fori_loop(0, 8, prepare, 0)

    for du in (1, 3, 2):
        block = at(zl, du, 0)
        it = item(block, g0, 2)
        recv(*it)
        send_item(it, near(v_devs))
        to_last(block).start()
        to_twin_core(block, g0, 2).start()
    block = at(other, 0, 0)
    it = item(block, g0 + 1, 1)
    recv(*it)
    send_item(it, near(u_devs) + near(v_devs))
    to_twin_core(block, g0 + 1, 1).start()
    recv(*item(block, g0, 1))
    to_twin_core(block, g0, 1).start()

    iq_all[pl.ds(pl.multiple_of(head * 64, 64), 64)] = iq_send[head]
    iw_recv[head] = iw_send[pl.ds(pl.multiple_of(head * 8, 8), 8)]
    for r in range(1, 8):
        d = (head + r) % 8
        recv(iq_all.at[pl.ds(pl.multiple_of(d * 64, 64), 64)], iq_sem.at[d])
        recv(iw_recv.at[d], iw_sem.at[d])
    for s in range(8):
        tile = iw_recv[s]
        for j in range(8):
            r = (s * 8 + j) * 8
            iw_all[r:r + 8, :] = jnp.broadcast_to(tile[:, j:j + 1], (8, 128))

    start0, start1 = bs_ref[0], bs_ref[1]

    def position(q):
        return jnp.where(q < 32, start0, start1) + q % 32

    def key_index(shape, par, half, w):
        sw, sj = 4 - 3 * half, 1 + 3 * half
        col = lax.broadcasted_iota(jnp.int32, shape, 1)
        return (par * 16 + w * sw) * 128 + half * 64 + (col // 64) * (sj * 128) + col % 64

    def chunk(par, half, w):
        sw, sj = 4 - 3 * half, 1 + 3 * half
        ci = par * 8 + half * 4 + w
        for j in range(4):
            block = par * 16 + w * sw + j * sj
            for g in range(2):
                r = j * 64 + g * 32
                packed = keys[block, 2 * half + g]
                kc[r:r + 16, 0:512] = packed[:, 0:512]
                ki[r:r + 16, :] = packed[:, 512:640]
                kc[r + 16:r + 32, 0:512] = packed[:, 640:1152]
                ki[r + 16:r + 32, :] = packed[:, 1152:1280]
                rope = packed[:, 1280:1408]
                kc[r:r + 16, 512:640] = rope
                kc[r + 16:r + 32, 512:640] = pltpu.roll(rope.astype(F32), 64, 1).astype(BF16)
        kct[...] = kc[...].T
        kit[...] = ki[...].T
        shape = (64, 256)
        seen = key_index(shape, par, half, w) <= position(lax.broadcasted_iota(jnp.int32, shape, 0))
        bias = jnp.where(seen, 0.0, NEG)

        def score(rb, carry):
            rows = pl.ds(pl.multiple_of(rb * SCORE_ROWS, SCORE_ROWS), SCORE_ROWS)
            s = jnp.dot(q_rows[rows], kct[...], preferred_element_type=F32)
            s = s.reshape(SCORE_ROWS // 64, 64, 256) + bias[None]
            expo[ci, rows] = s.reshape(SCORE_ROWS, 256)
            return carry

        lax.fori_loop(0, 1024 // SCORE_ROWS, score, 0)

        lg = jnp.zeros((8, 256), F32)
        for rb in range(2):
            rows = pl.ds(rb * 256, 256)
            s = jnp.dot(iq_all[rows], kit[...], preferred_element_type=F32)
            wt = iw_all[rows]
            s = jnp.maximum(s, 0.0) * jnp.concatenate([wt, wt], axis=1)
            lg = lg + jnp.sum(s.reshape(32, 8, 256), axis=0)
        lg = lg * INDEX_SCALE
        shape = (8, 256)
        seen = key_index(shape, par, half, w) <= position(
            head * 8 + lax.broadcasted_iota(jnp.int32, shape, 0)
        )
        logits[ci] = jnp.where(seen, lg, 0.0)

    def pair_base(half):
        return x + half * (y - x)

    def exponentials(par, half, pair, carry):
        base = pair_base(half)
        ca = par * 8 + half * 4 + lax.rem(base + 2 * pair, 4)
        cb = par * 8 + half * 4 + lax.rem(base + 2 * pair + 1, 4)
        sc = (par * 2 + half) * 2 + pair

        def block(rb, carry):
            rows = pl.ds(pl.multiple_of(rb * 64, 64), 64)
            refs = [(ca, 0), (ca, 128), (cb, 0), (cb, 128)]
            t = [expo[c, rows, l:l + 128] for c, l in refs]
            peak = jnp.maximum(jnp.maximum(t[0], t[1]), jnp.maximum(t[2], t[3]))
            e = [jnp.exp2((v - peak) * EXP_SCALE) for v in t]
            for (c, l), v in zip(refs, e):
                expo[c, rows, l:l + 128] = v
            peaks[sc, rows] = peak
            sums[sc, rows] = (e[0] + e[1]) + (e[2] + e[3])
            return carry

        return unrolled(16, 2, block, carry)

    def step(i, carry):
        t, side = lax.div(i, 2), lax.rem(i, 2)
        par_rel, turn = lax.div(t, 4), lax.rem(t, 4)
        pair = lax.div(turn, 2)
        du = turn + pair * (1 - 2 * lax.rem(turn, 2))
        half = core + side * (1 - 2 * core)
        par = zl + par_rel * (1 - 2 * zl)
        w = lax.rem(pair_base(half) + du, 4)

        @pl.when((side == 0) & (par_rel == 0))
        def _():
            for dv in (1, 3, 2):
                block = at(zl, du, dv)
                recv(*item(block, g0, 2))
                to_last(block).start()
                to_twin_core(block, g0, 2).start()

        @pl.when((side == 0) & (par_rel == 1))
        def _():
            for dv in ORDER:
                block = at(other, du, dv)

                def take_last(block=block):
                    recv(*item(block, g0, 1))
                    to_twin_core(block, g0, 1).start()

                if dv:
                    recv(*item(block, g0 + 1, 1))
                    to_twin_core(block, g0 + 1, 1).start()
                    take_last()
                else:
                    pl.when(du > 0)(take_last)

        @pl.when((side == 1) & (par_rel == 0))
        def _():
            for j in range(4):
                block = at(zl, j, du)

                def take(block=block):
                    recv(*item(block, 2 * twin_half, 2))

                if j:
                    take()
                else:
                    pl.when(du > 0)(take)

        @pl.when((side == 1) & (par_rel == 1))
        def _():
            for j in range(4):
                block = at(other, j, du)
                recv(*item(block, 2 * twin_half, 1))
                recv(*item(block, 2 * twin_half + 1, 1))

        chunk(par, half, w)

        @pl.when(i == 0)
        def _():
            for eu in (1, 3, 2):
                block = at(other, eu, 0)
                recv(*item(block, g0 + 1, 1))
                for copy in first_along_v(eu):
                    copy.start()
                to_twin_core(block, g0 + 1, 1).start()

        @pl.when(lax.rem(i, 4) == 3)
        def _():
            lax.fori_loop(0, 2, lambda h, c: exponentials(par, h, pair, c), 0)

        return carry

    lax.fori_loop(0, 16, step, 0)

    def normalise(rb, carry):
        rows = pl.ds(pl.multiple_of(rb * 64, 64), 64)
        m = [peaks[s, rows] for s in range(8)]
        top = jnp.max(functools.reduce(jnp.maximum, m), axis=1, keepdims=True)
        total = None
        for s in range(8):
            wt = jnp.exp2((m[s] - top) * EXP_SCALE)
            wts[s, rows] = wt
            part = sums[s, rows] * wt
            total = part if total is None else total + part
        share = 1.0 / (jnp.sum(total, axis=1, keepdims=True) * TEACHER_HEADS)
        for s in range(8):
            wts[s, rows] = wts[s, rows] * share
        return carry

    unrolled(16, 4, normalise, 0)

    def weigh(cp, d):
        parts = []
        for o in range(2):
            ci = cp * 2 + o
            sch = ci // 4
            half = sch % 2
            sc = sch * 2 + ((ci % 4 - pair_base(half) + 4) % 4) // 2
            acc = None
            for j in range(16):
                rows = pl.ds(pl.multiple_of(j * 64 + d * 8, 8), 8)
                wt = wts[sc, rows]
                term = expo[ci, rows] * jnp.concatenate([wt, wt], axis=1)
                acc = term if acc is None else acc + term
            parts.append(acc)
        return jnp.concatenate(parts, axis=0)

    for r in (1, 3, 2, 0):
        zi = (zh + r) % 4

        def to_twin(cp, carry):
            p_twin[zi, pl.ds(pl.multiple_of(cp * 16, 16), 16)] = weigh(cp, zi * 2 + 1 - core).astype(BF16)
            return carry

        lax.fori_loop(0, 8, to_twin, 0)
        send(p_twin.at[zi], p_twin_in.at[zi], twin_sem.at[zi], twin)

    for r in (1, 3, 2, 0):
        zi = (zh + r) % 4

        def mine(cp, carry):
            p_mine[cp] = weigh(cp, zi * 2 + core)
            return carry

        lax.fori_loop(0, 8, mine, 0)
        recv(p_twin_in.at[zi], twin_sem.at[zi])
        if r:

            def to_z(cp, carry):
                rows = pl.ds(pl.multiple_of(cp * 16, 16), 16)
                p_z[zi, rows] = (p_mine[cp] + p_twin_in[zi, rows].astype(F32)).astype(BF16)
                return carry

            lax.fori_loop(0, 8, to_z, 0)
            send(p_z.at[zi], p_z_in.at[zh], z_sem.at[zh], (ctx, zi * 2 + core))

    for j in range(8):
        par, xx = j // 4, j % 4
        for yy in range(4):
            a = logits[par * 8 + xx, :, 64 * yy:64 * yy + 64]
            b = logits[par * 8 + 4 + yy, :, 64 * xx:64 * xx + 64]
            lg_send[j, :, 128 * yy:128 * yy + 128] = jnp.concatenate([a, b], axis=1)
    for r, dev in enumerate(mates):
        send(lg_send.at[(head + r + 1) % 8], lg_all.at[head], lg_sem.at[head], dev)
    lg_all[head] = lg_send[head]

    shape = (8, 256)
    pos8 = position(head * 8 + lax.broadcasted_iota(jnp.int32, shape, 0))
    masked = []
    for ci in range(16):
        seen = key_index(shape, ci // 8, (ci // 4) % 2, ci % 4) <= pos8
        masked.append(jnp.where(seen, logits[ci], NEG))
    top = jnp.max(functools.reduce(jnp.maximum, masked), axis=1, keepdims=True)
    total = functools.reduce(jnp.add, [jnp.exp(v - top) for v in masked])
    lse = top + jnp.log(jnp.sum(total, axis=1, keepdims=True))

    for r in (1, 3, 2):
        recv(p_z_in.at[(zh + r) % 4], z_sem.at[(zh + r) % 4])

    def finish(cp, carry):
        rows = pl.ds(pl.multiple_of(cp * 16, 16), 16)
        p = p_mine[cp] + p_twin_in[zh, rows].astype(F32)
        for r in (1, 3, 2):
            p = p + p_z_in[(zh + r) % 4, rows].astype(F32)
        lg = jnp.concatenate([logits[cp * 2], logits[cp * 2 + 1]], axis=0)
        term = p * (jnp.log(jnp.where(p > 0, p, 1.0)) - lg)
        mass, cross = carry
        return mass + p[0:8] + p[8:16], cross + term[0:8] + term[8:16]

    zero = jnp.zeros((8, 256), F32)
    mass, cross = lax.fori_loop(0, 8, finish, (zero, zero))
    mass = jnp.sum(mass, axis=1, keepdims=True)
    div = jnp.sum(cross, axis=1, keepdims=True) / mass - jnp.log(mass) + lse
    div_all[head] = jnp.broadcast_to(div, (8, 128))
    for dev in mates:
        send(div_all.at[head], div_all.at[head], div_sem.at[head], dev)

    for r in range(1, 8):
        d = (head + r) % 8
        recv(lg_all.at[d], lg_sem.at[d])
    for d in range(8):
        out_ref[8 * d:8 * d + 8, :] = lg_all[d]
    for r in range(1, 8):
        d = (head + r) % 8
        recv(div_all.at[d], div_sem.at[d])
    for d in range(8):
        div_ref[8 * d:8 * d + 8, :] = div_all[d]
    for copy in sends:
        copy.wait_send()

    for eu in (1, 3, 2):
        for copy in first_along_v(eu):
            copy.wait_send()

    def drain(i, carry):
        du, dv = lax.div(i, 4), lax.rem(i, 4)
        block = at(zl, du, dv)
        to_last(block).wait_send()

        @pl.when(i > 0)
        def _():
            to_twin_core(block, g0, 2).wait_send()

        block = at(other, du, dv)
        to_twin_core(block, g0, 1).wait_send()
        to_twin_core(block, g0 + 1, 1).wait_send()
        return carry

    lax.fori_loop(0, 16, drain, 0)


def local(teacher_queries, latent_keys, index_queries, index_keys, index_weights, block_start):
    vmem = pl.BlockSpec(memory_space=pltpu.VMEM)
    dma = pltpu.SemaphoreType.DMA
    logits, div = pl.pallas_call(
        kernel,
        out_shape=(jax.ShapeDtypeStruct((64, 512), F32), jax.ShapeDtypeStruct((64, 128), F32)),
        in_specs=[
            pl.BlockSpec(memory_space=pl.ANY), vmem, vmem, vmem, vmem,
            pl.BlockSpec(memory_space=pltpu.SMEM),
        ],
        out_specs=(vmem, vmem),
        scratch_shapes=[
            pltpu.VMEM((64, 9216), BF16),
            pltpu.VMEM((1024, 640), BF16),
            pltpu.VMEM((32, 4, 16, 1408), BF16),
            pltpu.VMEM((256, 640), BF16),
            pltpu.VMEM((256, 128), BF16),
            pltpu.VMEM((640, 256), BF16),
            pltpu.VMEM((128, 256), BF16),
            pltpu.VMEM((16, 1024, 256), F32),
            pltpu.VMEM((8, 1024, 128), F32),
            pltpu.VMEM((8, 1024, 128), F32),
            pltpu.VMEM((8, 1024, 128), F32),
            pltpu.VMEM((8, 64, 128), BF16),
            pltpu.VMEM((512, 128), BF16),
            pltpu.VMEM((64, 128), F32),
            pltpu.VMEM((8, 8, 128), F32),
            pltpu.VMEM((512, 128), F32),
            pltpu.VMEM((16, 8, 256), F32),
            pltpu.VMEM((8, 8, 512), F32),
            pltpu.VMEM((8, 8, 512), F32),
            pltpu.VMEM((8, 16, 256), F32),
            pltpu.VMEM((4, 128, 256), BF16),
            pltpu.VMEM((4, 128, 256), BF16),
            pltpu.VMEM((4, 128, 256), BF16),
            pltpu.VMEM((4, 128, 256), BF16),
            pltpu.VMEM((8, 8, 128), F32),
            dma(()), dma((96,)), dma((32, 4)), dma((32,)), dma((4, 4)), dma((32, 4)), dma((8,)), dma((8,)), dma((8,)),
            dma((4,)), dma((4,)), dma((8,)),
        ],
        compiler_params=pltpu.CompilerParams(
            collective_id=0, has_side_effects=True, vmem_limit_bytes=56 << 20
        ),
    )(teacher_queries, latent_keys.T, index_queries, index_keys, index_weights.T, block_start)
    return logits, div[:, 0]


def solution(mesh):
    return jax.shard_map(
        local,
        mesh=mesh,
        in_specs=(
            P("ctx", "head"),
            P("ctx", None),
            P("ctx", "head"),
            P("ctx", None),
            P("ctx", "head"),
            P("ctx"),
        ),
        out_specs=(P("ctx", "head"), P("ctx")),
        check_vma=False,
    )
```

```python
import functools

import jax
import jax.numpy as jnp
from jax import lax
from jax.experimental import pallas as pl
from jax.experimental.pallas import tpu as pltpu
from jax.sharding import PartitionSpec as P

MESH = pl.DeviceIdType.MESH
F32, BF16 = jnp.float32, jnp.bfloat16
TEACHER_HEADS = 128
LATENT, ROPE, WIDTH, IDIM = 512, 64, 576, 128
NEG = -1e30
EXP_ROWS = 256
EXP_SCALE = 192.0 ** (-0.5) * 1.4426950408889634
INDEX_SCALE = 128.0 ** (-0.5)
ORDER = (0, 1, 3, 2)


def unrolled(n, by, body, carry):
    def several(i, carry):
        for u in range(by):
            carry = body(i * by + u, carry)
        return carry

    return lax.fori_loop(0, n // by, several, carry)


def kernel(
    tq_hbm, lk_ref, iq_ref, ik_ref, iw_ref, bs_ref,
    out_ref, div_ref,
    tq, q_rows, keys, kc, ki, kct, kit, raw, expo, peaks, sums, wts,
    iq_send, iq_all, iw_send, iw_recv, iw_all, logits, lg_send, lg_all,
    p_mine, p_twin, p_twin_in, p_z, p_z_in, div_all,
    copy_sem, send_sem, twin_out, z_out, v_out, lg_out, key_sem, iq_sem, iw_sem, lg_sem, twin_sem, z_sem, div_sem,
):
    ctx, head = lax.axis_index("ctx"), lax.axis_index("head")
    zl, x, y = ctx // 16, (ctx // 4) % 4, ctx % 4
    zh, core = head // 2, head % 2
    z = zh * 2 + zl
    pu, pv = x + core * (y - x), y + core * (x - y)
    twin = (ctx, zh * 2 + 1 - core)

    def ctx_of(par, u, v):
        u, v = lax.rem(u, 4), lax.rem(v, 4)
        return par * 16 + (u + core * (v - u)) * 4 + v + core * (u - v)

    def z_device(dz):
        zz = (z + dz + 8) % 8
        return ((zz % 2) * 16 + x * 4 + y, (zz // 2) * 2 + core)

    u_devs = {d: (ctx_of(zl, pu + d, pv), head) for d in (1, 3, 2)}
    v_devs = {d: (ctx_of(zl, pu, pv + d), head) for d in (1, 3, 2)}
    first_dev = z_device(2 * core - 1)
    last_dev = z_device(1 - 2 * core)
    mates = [(ctx, (head + r) % 8) for r in range(1, 8)]

    tq_copy = pltpu.make_async_copy(tq_hbm, tq, copy_sem)
    tq_copy.start()

    barrier = pltpu.get_barrier_semaphore()
    partners = list(u_devs.values()) + list(v_devs.values()) + [first_dev, last_dev] + mates
    for dev in partners:
        pl.semaphore_signal(barrier, inc=1, device_id=dev, device_id_type=MESH)

    lat = [lk_ref[128 * t:128 * t + 128, :].T for t in range(4)]
    rope = jnp.concatenate([lk_ref[512:576, :].astype(F32), jnp.zeros((64, 128), F32)], axis=0).T
    for g in range(4):
        a, b = g * 32, g * 32 + 16
        for t in range(4):
            keys[ctx, g, :, 128 * t:128 * t + 128] = lat[t][a:a + 16]
            keys[ctx, g, :, 640 + 128 * t:768 + 128 * t] = lat[t][b:b + 16]
        keys[ctx, g, :, 512:640] = ik_ref[a:a + 16, :]
        keys[ctx, g, :, 1152:1280] = ik_ref[b:b + 16, :]
        keys[ctx, g, :, 1280:1408] = (rope[a:a + 16] + pltpu.roll(rope[b:b + 16], 64, 1)).astype(BF16)

    iqf = iq_ref[...].astype(F32)
    for d in range(8):
        iq_send[d] = jnp.concatenate(
            [iqf[8 * d:8 * d + 8, 128 * j:128 * j + 128] for j in range(8)], axis=0
        ).astype(BF16)
    weights = jnp.concatenate([iw_ref[...].astype(F32), jnp.zeros((8, 64), F32)], axis=1)
    weights = jnp.concatenate([weights, jnp.zeros((120, 128), F32)], axis=0).T
    iw_send[...] = weights[0:64]

    pl.semaphore_wait(barrier, len(partners))

    sends = []

    def remote(src, dst, out_sem, in_sem, dev):
        return pltpu.make_async_remote_copy(
            src_ref=src, dst_ref=dst, send_sem=out_sem, recv_sem=in_sem,
            device_id=dev, device_id_type=MESH,
        )

    def send(src, dst, in_sem, dev):
        copy = remote(src, dst, send_sem.at[len(sends)], in_sem, dev)
        copy.start()
        sends.append(copy)

    def recv(dst, in_sem):
        remote(dst, dst, send_sem.at[0], in_sem, twin).wait_recv()

    def item(block, group, n):
        return keys.at[block, pl.ds(group, n)], key_sem.at[block, group]

    def send_item(it, devs):
        for dev in devs:
            send(it[0], it[0], it[1], dev)

    def to_twin_core(block):
        ref = keys.at[block, pl.ds(g0, 2)]
        return remote(ref, ref, twin_out.at[block], key_sem.at[block, g0], twin)

    def along_z(block):
        copies = []
        for g, dev in ((0, last_dev), (1, first_dev)):
            ref = keys.at[block, pl.ds(g0 + g, 1)]
            copies.append(remote(ref, ref, z_out.at[block, g], key_sem.at[block, g0 + g], dev))
        return copies

    def along_v(par_rel, du):
        block = at(zl + par_rel * (1 - 2 * zl), du, 0)
        ref = keys.at[block, pl.ds(g0, 2)]
        return [
            remote(ref, ref, v_out.at[par_rel * 4 + du, dv], key_sem.at[block, g0], v_devs[dv])
            for dv in (1, 3, 2)
        ]

    near = lambda devs: [devs[1], devs[3], devs[2]]
    g0 = 2 * core
    other = 1 - zl
    twin_half = 1 - core
    at = lambda par, du, dv: ctx_of(par, pu + du, pv + dv)

    send_item(item(ctx, g0, 2), near(u_devs))
    for copy in along_z(ctx):
        copy.start()
    for r, dev in enumerate(mates):
        d = (head + r + 1) % 8
        send(iq_send.at[d], iq_all.at[pl.ds(pl.multiple_of(head * 64, 64), 64)], iq_sem.at[head], dev)
        send(iw_send.at[pl.ds(pl.multiple_of(d * 8, 8), 8)], iw_recv.at[head], iw_sem.at[head], dev)

    tq_copy.wait()
    lane = lax.broadcasted_iota(jnp.int32, (64, 128), 1)

    def prepare(i, carry):
        base = pl.multiple_of(i * 1152, 128)
        row = pl.multiple_of(i * 128, 128)
        q_rows[pl.ds(row, 64), 0:512] = tq[:, pl.ds(base, 512)]
        tiles = [tq[:, pl.ds(base + 512 + 128 * t, 128)].astype(F32) for t in range(5)]
        q_rows[pl.ds(row, 64), 512:640] = jnp.where(lane < 64, tiles[0], 0.0).astype(BF16)
        rolled = [pltpu.roll(t, 64, 1) for t in tiles]
        rolled.append(jnp.zeros_like(rolled[0]))
        for t in range(5):
            q_rows[pl.ds(row + 64, 64), 128 * t:128 * t + 128] = jnp.where(
                lane < 64, rolled[t], rolled[t + 1]
            ).astype(BF16)
        return carry

    for copy in along_v(0, 0):
        copy.start()
    lax.fori_loop(0, 8, prepare, 0)

    def from_z(du):
        block = at(other, du, 0)
        for g in range(2):
            recv(*item(block, g0 + g, 1))
        for copy in along_v(1, du):
            copy.start()
        to_twin_core(block).start()

    for du in (1, 3, 2):
        block = at(zl, du, 0)
        recv(*item(block, g0, 2))
        for copy in along_z(block):
            copy.start()
        if du == 1:
            from_z(0)
        for copy in along_v(0, du):
            copy.start()
        to_twin_core(block).start()

    iq_all[pl.ds(pl.multiple_of(head * 64, 64), 64)] = iq_send[head]
    iw_recv[head] = iw_send[pl.ds(pl.multiple_of(head * 8, 8), 8)]
    for r in range(1, 8):
        d = (head + r) % 8
        recv(iq_all.at[pl.ds(pl.multiple_of(d * 64, 64), 64)], iq_sem.at[d])
        recv(iw_recv.at[d], iw_sem.at[d])
    for s in range(8):
        tile = iw_recv[s]
        for j in range(8):
            r = (s * 8 + j) * 8
            iw_all[r:r + 8, :] = jnp.broadcast_to(tile[:, j:j + 1], (8, 128))

    start0, start1 = bs_ref[0], bs_ref[1]

    def position(q):
        return jnp.where(q < 32, start0, start1) + q % 32

    def key_index(shape, par, half, w):
        sw, sj = 4 - 3 * half, 1 + 3 * half
        col = lax.broadcasted_iota(jnp.int32, shape, 1)
        return (par * 16 + w * sw) * 128 + half * 64 + (col // 64) * (sj * 128) + col % 64

    def assemble(slot, par, half, w):
        sw, sj = 4 - 3 * half, 1 + 3 * half
        for j in range(4):
            block = par * 16 + w * sw + j * sj
            for g in range(2):
                r = j * 64 + g * 32
                packed = keys[block, 2 * half + g]
                kc[slot, r:r + 16, 0:512] = packed[:, 0:512]
                ki[slot, r:r + 16, :] = packed[:, 512:640]
                kc[slot, r + 16:r + 32, 0:512] = packed[:, 640:1152]
                ki[slot, r + 16:r + 32, :] = packed[:, 1152:1280]
                rope = packed[:, 1280:1408]
                kc[slot, r:r + 16, 512:640] = rope
                kc[slot, r + 16:r + 32, 512:640] = pltpu.roll(rope.astype(F32), 64, 1).astype(BF16)
        kct[slot] = kc[slot].T
        kit[slot] = ki[slot].T

    def chunk(slot, held, par, half, w):
        ci = par * 8 + half * 4 + w
        shape = (64, 256)
        seen = key_index(shape, par, half, w) <= position(lax.broadcasted_iota(jnp.int32, shape, 0))
        bias = jnp.where(seen, 0.0, NEG)
        scores = jnp.dot(q_rows[...], kct[slot], preferred_element_type=F32)
        raw[held] = (scores.reshape(16, 64, 256) + bias[None]).reshape(1024, 256)

        s = jnp.dot(iq_all[...], kit[slot], preferred_element_type=F32)
        wt = iw_all[...]
        s = jnp.maximum(s, 0.0) * jnp.concatenate([wt, wt], axis=1)
        lg = jnp.sum(s.reshape(64, 8, 256), axis=0) * INDEX_SCALE
        shape = (8, 256)
        seen = key_index(shape, par, half, w) <= position(
            head * 8 + lax.broadcasted_iota(jnp.int32, shape, 0)
        )
        logits[ci] = jnp.where(seen, lg, 0.0)

    def pair_base(half):
        return x + half * (y - x)

    def exponentials(held, par, half, pair):
        base = pair_base(half)
        ca = par * 8 + half * 4 + lax.rem(base + 3 * pair, 4)
        cb = par * 8 + half * 4 + lax.rem(base + 1 + pair, 4)
        sc = (par * 2 + half) * 2 + pair
        held = held + 2 * half

        def block(rb, carry):
            rows = pl.ds(pl.multiple_of(rb * EXP_ROWS, EXP_ROWS), EXP_ROWS)
            refs = [(0, ca, 0), (0, ca, 128), (1, cb, 0), (1, cb, 128)]
            t = [raw[held + o, rows, l:l + 128] for o, _, l in refs]
            peak = jnp.maximum(jnp.maximum(t[0], t[1]), jnp.maximum(t[2], t[3]))
            e = [jnp.exp2((v - peak) * EXP_SCALE) for v in t]
            for (_, c, l), v in zip(refs, e):
                expo[c, rows, l:l + 128] = v
            peaks[sc, rows] = peak
            sums[sc, rows] = (e[0] + e[1]) + (e[2] + e[3])
            return carry

        lax.fori_loop(0, 1024 // EXP_ROWS, block, 0)

    def logits_copy(j):
        return remote(lg_send.at[j], lg_all.at[head], lg_out.at[j], lg_sem.at[head], (ctx, j))

    def send_logits(par):
        for xx in range(4):
            j = par * 4 + xx
            for yy in range(4):
                a = logits[par * 8 + xx, :, 64 * yy:64 * yy + 64]
                b = logits[par * 8 + 4 + yy, :, 64 * xx:64 * xx + 64]
                lg_send[j, :, 128 * yy:128 * yy + 128] = jnp.concatenate([a, b], axis=1)

            @pl.when(j != head)
            def _():
                logits_copy(j).start()

            @pl.when(j == head)
            def _():
                lg_all[head] = lg_send[j]

    def step(i, carry):
        par_rel = jnp.where((i == 1) | (i >= 5), 1, 0)
        turn = jnp.where(i < 2, 0, jnp.where(i < 5, i - 1, i - 4))
        pair = lax.div(turn, 2)
        du = turn + pair * (1 - 2 * lax.rem(turn, 2))
        par = zl + par_rel * (1 - 2 * zl)
        w_mine = lax.rem(pair_base(core) + du, 4)
        w_twin = lax.rem(pair_base(twin_half) + du, 4)

        for dv in (1, 3, 2):
            block = at(par, du, dv)
            recv(*item(block, g0, 2))
            to_twin_core(block).start()

        @pl.when(i < 3)
        def _():
            from_z(jnp.where(i == 0, 1, 4 - i))

        assemble(0, par, core, w_mine)
        held = par_rel * 4 + lax.rem(turn, 2)
        chunk(0, held + 2 * core, par, core, w_mine)

        for j in range(4):
            block = at(par, j, du)

            def take(block=block):
                recv(*item(block, 2 * twin_half, 2))

            if j:
                take()
            else:
                pl.when(i > 0)(take)

        assemble(1, par, twin_half, w_twin)
        chunk(1, held + 2 * twin_half, par, twin_half, w_twin)

        @pl.when(lax.rem(turn, 2) == 1)
        def _():
            exponentials(par_rel * 4, par, 0, pair)
            exponentials(par_rel * 4, par, 1, pair)

        @pl.when(turn == 3)
        def _():
            send_logits(par)

        return carry

    lax.fori_loop(0, 8, step, 0)

    def normalise(rb, carry):
        rows = pl.ds(pl.multiple_of(rb * 128, 128), 128)
        m = [peaks[s, rows] for s in range(8)]
        top = jnp.max(functools.reduce(jnp.maximum, m), axis=1, keepdims=True)
        w = [jnp.exp2((v - top) * EXP_SCALE) for v in m]
        total = functools.reduce(jnp.add, [sums[s, rows] * w[s] for s in range(8)])
        share = 1.0 / (jnp.sum(total, axis=1, keepdims=True) * TEACHER_HEADS)
        for s in range(8):
            wts[s, rows] = w[s] * share
        return carry

    lax.fori_loop(0, 8, normalise, 0)

    def weigh(cp, d):
        parts = []
        for o in range(2):
            ci = cp * 2 + o
            sch = ci // 4
            half = sch % 2
            sc = sch * 2 + ((ci % 4 - pair_base(half) + 4) % 4) // 2
            acc = None
            for j in range(16):
                rows = pl.ds(pl.multiple_of(j * 64 + d * 8, 8), 8)
                wt = wts[sc, rows]
                term = expo[ci, rows] * jnp.concatenate([wt, wt], axis=1)
                acc = term if acc is None else acc + term
            parts.append(acc)
        return jnp.concatenate(parts, axis=0)

    for r in (1, 3, 2, 0):
        zi = (zh + r) % 4

        def to_twin(cp, carry):
            p_twin[zi, pl.ds(pl.multiple_of(cp * 16, 16), 16)] = weigh(cp, zi * 2 + 1 - core).astype(BF16)
            return carry

        lax.fori_loop(0, 8, to_twin, 0)
        send(p_twin.at[zi], p_twin_in.at[zi], twin_sem.at[zi], twin)

    for r in (1, 3, 2, 0):
        zi = (zh + r) % 4

        def mine(cp, carry):
            p_mine[cp] = weigh(cp, zi * 2 + core)
            return carry

        lax.fori_loop(0, 8, mine, 0)
        recv(p_twin_in.at[zi], twin_sem.at[zi])
        if r:

            def to_z(cp, carry):
                rows = pl.ds(pl.multiple_of(cp * 16, 16), 16)
                p_z[zi, rows] = (p_mine[cp] + p_twin_in[zi, rows].astype(F32)).astype(BF16)
                return carry

            lax.fori_loop(0, 8, to_z, 0)
            send(p_z.at[zi], p_z_in.at[zh], z_sem.at[zh], (ctx, zi * 2 + core))

    shape = (8, 256)
    pos8 = position(head * 8 + lax.broadcasted_iota(jnp.int32, shape, 0))
    masked = []
    for ci in range(16):
        seen = key_index(shape, ci // 8, (ci // 4) % 2, ci % 4) <= pos8
        masked.append(jnp.where(seen, logits[ci], NEG))
    top = jnp.max(functools.reduce(jnp.maximum, masked), axis=1, keepdims=True)
    total = functools.reduce(jnp.add, [jnp.exp(v - top) for v in masked])
    lse = top + jnp.log(jnp.sum(total, axis=1, keepdims=True))

    for r in (1, 3, 2):
        recv(p_z_in.at[(zh + r) % 4], z_sem.at[(zh + r) % 4])

    def finish(cp, carry):
        rows = pl.ds(pl.multiple_of(cp * 16, 16), 16)
        p = p_mine[cp] + p_twin_in[zh, rows].astype(F32)
        for r in (1, 3, 2):
            p = p + p_z_in[(zh + r) % 4, rows].astype(F32)
        lg = jnp.concatenate([logits[cp * 2], logits[cp * 2 + 1]], axis=0)
        term = p * (jnp.log(jnp.where(p > 0, p, 1.0)) - lg)
        mass, cross = carry
        return mass + p[0:8] + p[8:16], cross + term[0:8] + term[8:16]

    zero = jnp.zeros((8, 256), F32)
    mass, cross = lax.fori_loop(0, 8, finish, (zero, zero))
    mass = jnp.sum(mass, axis=1, keepdims=True)
    div = jnp.sum(cross, axis=1, keepdims=True) / mass - jnp.log(mass) + lse
    div_all[head] = jnp.broadcast_to(div, (8, 128))
    for dev in mates:
        send(div_all.at[head], div_all.at[head], div_sem.at[head], dev)

    for r in range(1, 8):
        d = (head + r) % 8
        recv(lg_all.at[d], lg_sem.at[d])
    for d in range(8):
        out_ref[8 * d:8 * d + 8, :] = lg_all[d]
    for r in range(1, 8):
        d = (head + r) % 8
        recv(div_all.at[d], div_sem.at[d])
    column = jnp.concatenate([div_all[d] for d in range(8)] + [jnp.zeros((64, 128), F32)], axis=0)
    div_ref[...] = column.T[0:8]
    for copy in sends:
        copy.wait_send()

    for du in range(4):
        for copy in along_z(at(zl, du, 0)) + along_v(0, du) + along_v(1, du):
            copy.wait_send()
    for r in range(1, 8):
        logits_copy(lax.rem(head + r, 8)).wait_send()

    def drain(i, carry):
        block = lax.rem(ctx + i, 32)
        to_twin_core(block).wait_send()
        return carry

    lax.fori_loop(1, 32, drain, 0)


def hand_over(logits_ref, div_ref, out_ref, out_div_ref):
    out_ref[...] = logits_ref[...]
    out_div_ref[...] = div_ref[0:1, 0:64]


def local(teacher_queries, latent_keys, index_queries, index_keys, index_weights, block_start):
    vmem = pl.BlockSpec(memory_space=pltpu.VMEM)
    dma = pltpu.SemaphoreType.DMA
    logits, div = pl.pallas_call(
        kernel,
        out_shape=(jax.ShapeDtypeStruct((64, 512), F32), jax.ShapeDtypeStruct((8, 128), F32)),
        in_specs=[
            pl.BlockSpec(memory_space=pl.ANY), vmem, vmem, vmem, vmem,
            pl.BlockSpec(memory_space=pltpu.SMEM),
        ],
        out_specs=(vmem, vmem),
        scratch_shapes=[
            pltpu.VMEM((64, 9216), BF16),
            pltpu.VMEM((1024, 640), BF16),
            pltpu.VMEM((32, 4, 16, 1408), BF16),
            pltpu.VMEM((2, 256, 640), BF16),
            pltpu.VMEM((2, 256, 128), BF16),
            pltpu.VMEM((2, 640, 256), BF16),
            pltpu.VMEM((2, 128, 256), BF16),
            pltpu.VMEM((8, 1024, 256), F32),
            pltpu.VMEM((16, 1024, 256), F32),
            pltpu.VMEM((8, 1024, 128), F32),
            pltpu.VMEM((8, 1024, 128), F32),
            pltpu.VMEM((8, 1024, 128), F32),
            pltpu.VMEM((8, 64, 128), BF16),
            pltpu.VMEM((512, 128), BF16),
            pltpu.VMEM((64, 128), F32),
            pltpu.VMEM((8, 8, 128), F32),
            pltpu.VMEM((512, 128), F32),
            pltpu.VMEM((16, 8, 256), F32),
            pltpu.VMEM((8, 8, 512), F32),
            pltpu.VMEM((8, 8, 512), F32),
            pltpu.VMEM((8, 16, 256), F32),
            pltpu.VMEM((4, 128, 256), BF16),
            pltpu.VMEM((4, 128, 256), BF16),
            pltpu.VMEM((4, 128, 256), BF16),
            pltpu.VMEM((4, 128, 256), BF16),
            pltpu.VMEM((8, 8, 128), F32),
            dma(()), dma((96,)), dma((32,)), dma((32, 2)), dma((8, 4)), dma((8,)), dma((32, 4)), dma((8,)), dma((8,)), dma((8,)),
            dma((4,)), dma((4,)), dma((8,)),
        ],
        compiler_params=pltpu.CompilerParams(
            collective_id=0, has_side_effects=True, vmem_limit_bytes=56 << 20
        ),
    )(teacher_queries, latent_keys.T, index_queries, index_keys, index_weights.T, block_start)
    logits, div = pl.pallas_call(
        hand_over,
        out_shape=(jax.ShapeDtypeStruct((64, 512), F32), jax.ShapeDtypeStruct((1, 64), F32)),
        in_specs=[vmem, vmem],
        out_specs=(vmem, vmem),
    )(logits, div)
    return logits, div.reshape(64)


def solution(mesh):
    return jax.shard_map(
        local,
        mesh=mesh,
        in_specs=(
            P("ctx", "head"),
            P("ctx", None),
            P("ctx", "head"),
            P("ctx", None),
            P("ctx", "head"),
            P("ctx"),
        ),
        out_specs=(P("ctx", "head"), P("ctx")),
        check_vma=False,
    )
```

```python
import functools

import jax
import jax.numpy as jnp
from jax import lax
from jax.experimental import pallas as pl
from jax.experimental.pallas import tpu as pltpu
from jax.sharding import PartitionSpec as P

MESH = pl.DeviceIdType.MESH
F32, BF16 = jnp.float32, jnp.bfloat16
TEACHER_HEADS = 128
LATENT, ROPE, WIDTH, IDIM = 512, 64, 576, 128
NEG = -1e30
EXP_ROWS = 256
EXP_SCALE = 192.0 ** (-0.5) * 1.4426950408889634
INDEX_SCALE = 128.0 ** (-0.5)
ORDER = (0, 1, 3, 2)


def unrolled(n, by, body, carry):
    def several(i, carry):
        for u in range(by):
            carry = body(i * by + u, carry)
        return carry

    return lax.fori_loop(0, n // by, several, carry)


def kernel(
    tq_hbm, lk_ref, iq_ref, ik_ref, iw_ref, bs_ref,
    out_ref, div_ref,
    tq, q_rows, keys, kc, ki, kct, kit, raw, expo, peaks, sums, wts,
    iq_send, iq_all, iw_send, iw_recv, iw_all, logits, lg_send, lg_all,
    p_mine, p_twin, p_twin_in, p_z, p_z_in, div_all,
    copy_sem, send_sem, twin_out, first_out, v_out, row_out, turn_out, lg_out, row_sem, col_sem, turn_sem, twin_in, iq_sem, iw_sem, lg_sem, twin_sem, z_sem, div_sem,
):
    ctx, head = lax.axis_index("ctx"), lax.axis_index("head")
    zl, x, y = ctx // 16, (ctx // 4) % 4, ctx % 4
    zh, core = head // 2, head % 2
    z = zh * 2 + zl
    pu, pv = x + core * (y - x), y + core * (x - y)
    twin = (ctx, zh * 2 + 1 - core)

    def ctx_of(par, u, v):
        u, v = lax.rem(u, 4), lax.rem(v, 4)
        return par * 16 + (u + core * (v - u)) * 4 + v + core * (u - v)

    def z_device(dz):
        zz = (z + dz + 8) % 8
        return ((zz % 2) * 16 + x * 4 + y, (zz // 2) * 2 + core)

    u_devs = {d: (ctx_of(zl, pu + d, pv), head) for d in (1, 3, 2)}
    v_devs = {d: (ctx_of(zl, pu, pv + d), head) for d in (1, 3, 2)}
    first_dev = z_device(2 * core - 1)
    last_dev = z_device(1 - 2 * core)
    mates = [(ctx, (head + r) % 8) for r in range(1, 8)]

    tq_copy = pltpu.make_async_copy(tq_hbm, tq, copy_sem)
    tq_copy.start()

    barrier = pltpu.get_barrier_semaphore()
    partners = list(u_devs.values()) + list(v_devs.values()) + [first_dev, last_dev] + mates
    for dev in partners:
        pl.semaphore_signal(barrier, inc=1, device_id=dev, device_id_type=MESH)

    lat = [lk_ref[128 * t:128 * t + 128, :].T for t in range(4)]
    rope = jnp.concatenate([lk_ref[512:576, :].astype(F32), jnp.zeros((64, 128), F32)], axis=0).T
    for g in range(4):
        a, b = g * 32, g * 32 + 16
        for t in range(4):
            keys[zl, x, y, g, :, 128 * t:128 * t + 128] = lat[t][a:a + 16]
            keys[zl, x, y, g, :, 640 + 128 * t:768 + 128 * t] = lat[t][b:b + 16]
        keys[zl, x, y, g, :, 512:640] = ik_ref[a:a + 16, :]
        keys[zl, x, y, g, :, 1152:1280] = ik_ref[b:b + 16, :]
        keys[zl, x, y, g, :, 1280:1408] = (rope[a:a + 16] + pltpu.roll(rope[b:b + 16], 64, 1)).astype(BF16)

    pl.semaphore_wait(barrier, len(partners))

    sends = []

    def remote(src, dst, out_sem, in_sem, dev):
        return pltpu.make_async_remote_copy(
            src_ref=src, dst_ref=dst, send_sem=out_sem, recv_sem=in_sem,
            device_id=dev, device_id_type=MESH,
        )

    def send(src, dst, in_sem, dev):
        copy = remote(src, dst, send_sem.at[len(sends)], in_sem, dev)
        copy.start()
        sends.append(copy)

    def recv(dst, in_sem):
        remote(dst, dst, send_sem.at[0], in_sem, twin).wait_recv()

    def copies(ref, out_sem, in_sem, dev):
        return remote(ref, ref, out_sem, in_sem, dev)

    def part(par, u, v, group=0, n=2):
        u, v = lax.rem(u, 4), lax.rem(v, 4)
        return keys.at[par, u + core * (v - u), v + core * (u - v), pl.ds(g0 + group, n)]

    def turn_part(which, par, u, group, n):
        u = lax.rem(u, 4)
        if which == 0:
            return keys.at[par, u, :, pl.ds(g0 + group, n)]
        return keys.at[par, :, u, pl.ds(g0 + group, n)]

    def by_core(start):
        for which in range(2):
            pl.when(core == which)(functools.partial(start, which))

    def along_v(par_rel, du):
        par = zl + par_rel * (1 - 2 * zl)
        return [
            copies(part(par, pu + du, pv), v_out.at[par_rel * 4 + du, dv],
                   col_sem.at[par, lax.rem(pu + du, 4)], v_devs[dv])
            for dv in (1, 3, 2)
        ]

    def row_along_z(du):
        return [
            copies(part(zl, pu + du, pv, g, 1), row_out.at[du, g],
                   row_sem.at[zl, lax.rem(pu + du, 4), 1 + g], dev)
            for g, dev in ((0, last_dev), (1, first_dev))
        ]

    def turn_along_z(which, du):
        return [
            copies(turn_part(which, zl, pu + du, g, 1), turn_out.at[du, g],
                   turn_sem.at[zl, lax.rem(pu + du, 4), g], dev)
            for g, dev in ((0, last_dev), (1, first_dev))
        ]

    def turn_to_twin(which, par_rel, du):
        par = zl + par_rel * (1 - 2 * zl)
        return copies(turn_part(which, par, pu + du, 0, 2), twin_out.at[par_rel * 4 + du],
                      twin_in.at[par, lax.rem(pu + du, 4)], twin)

    def first_to_twin(dv):
        return copies(part(zl, pu, pv + dv), first_out.at[dv], twin_in.at[zl, pu], twin)

    def start_all(several):
        for copy in several:
            copy.start()

    near = lambda devs: [devs[1], devs[3], devs[2]]
    g0 = 2 * core
    other = 1 - zl
    twin_half = 1 - core
    for dev in near(u_devs):
        send(part(zl, pu, pv), part(zl, pu, pv), row_sem.at[zl, pu, 0], dev)

    iqf = iq_ref[...].astype(F32)
    for d in range(8):
        iq_send[d] = jnp.concatenate(
            [iqf[8 * d:8 * d + 8, 128 * j:128 * j + 128] for j in range(8)], axis=0
        ).astype(BF16)
    weights = jnp.concatenate([iw_ref[...].astype(F32), jnp.zeros((8, 64), F32)], axis=1)
    weights = jnp.concatenate([weights, jnp.zeros((120, 128), F32)], axis=0).T
    iw_send[...] = weights[0:64]

    for r, dev in enumerate(mates):
        d = (head + r + 1) % 8
        send(iq_send.at[d], iq_all.at[pl.ds(pl.multiple_of(head * 64, 64), 64)], iq_sem.at[head], dev)
        send(iw_send.at[pl.ds(pl.multiple_of(d * 8, 8), 8)], iw_recv.at[head], iw_sem.at[head], dev)

    tq_copy.wait()
    lane = lax.broadcasted_iota(jnp.int32, (64, 128), 1)

    def prepare(i, carry):
        base = pl.multiple_of(i * 1152, 128)
        row = pl.multiple_of(i * 128, 128)
        q_rows[pl.ds(row, 64), 0:512] = tq[:, pl.ds(base, 512)]
        tiles = [tq[:, pl.ds(base + 512 + 128 * t, 128)].astype(F32) for t in range(5)]
        q_rows[pl.ds(row, 64), 512:640] = jnp.where(lane < 64, tiles[0], 0.0).astype(BF16)
        rolled = [pltpu.roll(t, 64, 1) for t in tiles]
        rolled.append(jnp.zeros_like(rolled[0]))
        for t in range(5):
            q_rows[pl.ds(row + 64, 64), 128 * t:128 * t + 128] = jnp.where(
                lane < 64, rolled[t], rolled[t + 1]
            ).astype(BF16)
        return carry

    start_all(along_v(0, 0))
    lax.fori_loop(0, 8, prepare, 0)

    for du in (1, 3, 2):
        recv(part(zl, pu + du, pv), row_sem.at[zl, lax.rem(pu + du, 4), 0])
        if du != 1:
            start_all(row_along_z(du))
        start_all(along_v(0, du))

    iq_all[pl.ds(pl.multiple_of(head * 64, 64), 64)] = iq_send[head]
    iw_recv[head] = iw_send[pl.ds(pl.multiple_of(head * 8, 8), 8)]
    for r in range(1, 8):
        d = (head + r) % 8
        recv(iq_all.at[pl.ds(pl.multiple_of(d * 64, 64), 64)], iq_sem.at[d])
        recv(iw_recv.at[d], iw_sem.at[d])
    for s in range(8):
        tile = iw_recv[s]
        for j in range(8):
            r = (s * 8 + j) * 8
            iw_all[r:r + 8, :] = jnp.broadcast_to(tile[:, j:j + 1], (8, 128))

    start0, start1 = bs_ref[0], bs_ref[1]

    def position(q):
        return jnp.where(q < 32, start0, start1) + q % 32

    def key_index(shape, par, half, w):
        sw, sj = 4 - 3 * half, 1 + 3 * half
        col = lax.broadcasted_iota(jnp.int32, shape, 1)
        return (par * 16 + w * sw) * 128 + half * 64 + (col // 64) * (sj * 128) + col % 64

    def assemble(slot, par, half, w):
        for j in range(4):
            kx, ky = w + half * (j - w), j + half * (w - j)
            for g in range(2):
                r = j * 64 + g * 32
                packed = keys[par, kx, ky, 2 * half + g]
                kc[slot, r:r + 16, 0:512] = packed[:, 0:512]
                ki[slot, r:r + 16, :] = packed[:, 512:640]
                kc[slot, r + 16:r + 32, 0:512] = packed[:, 640:1152]
                ki[slot, r + 16:r + 32, :] = packed[:, 1152:1280]
                rope = packed[:, 1280:1408]
                kc[slot, r:r + 16, 512:640] = rope
                kc[slot, r + 16:r + 32, 512:640] = pltpu.roll(rope.astype(F32), 64, 1).astype(BF16)
        kct[slot] = kc[slot].T
        kit[slot] = ki[slot].T

    def chunk(slot, held, par, half, w):
        ci = par * 8 + half * 4 + w
        shape = (64, 256)
        seen = key_index(shape, par, half, w) <= position(lax.broadcasted_iota(jnp.int32, shape, 0))
        bias = jnp.where(seen, 0.0, NEG)
        scores = jnp.dot(q_rows[...], kct[slot], preferred_element_type=F32)
        raw[held] = (scores.reshape(16, 64, 256) + bias[None]).reshape(1024, 256)

        s = jnp.dot(iq_all[...], kit[slot], preferred_element_type=F32)
        wt = iw_all[...]
        s = jnp.maximum(s, 0.0) * jnp.concatenate([wt, wt], axis=1)
        lg = jnp.sum(s.reshape(64, 8, 256), axis=0) * INDEX_SCALE
        shape = (8, 256)
        seen = key_index(shape, par, half, w) <= position(
            head * 8 + lax.broadcasted_iota(jnp.int32, shape, 0)
        )
        logits[ci] = jnp.where(seen, lg, 0.0)

    def pair_base(half):
        return x + half * (y - x)

    def exponentials(held, par, half, pair):
        base = pair_base(half)
        ca = par * 8 + half * 4 + lax.rem(base + 3 * pair, 4)
        cb = par * 8 + half * 4 + lax.rem(base + 1 + pair, 4)
        sc = (par * 2 + half) * 2 + pair
        held = held + 2 * half

        def block(rb, carry):
            rows = pl.ds(pl.multiple_of(rb * EXP_ROWS, EXP_ROWS), EXP_ROWS)
            refs = [(0, ca, 0), (0, ca, 128), (1, cb, 0), (1, cb, 128)]
            t = [raw[held + o, rows, l:l + 128] for o, _, l in refs]
            peak = jnp.maximum(jnp.maximum(t[0], t[1]), jnp.maximum(t[2], t[3]))
            e = [jnp.exp2((v - peak) * EXP_SCALE) for v in t]
            for (_, c, l), v in zip(refs, e):
                expo[c, rows, l:l + 128] = v
            peaks[sc, rows] = peak
            sums[sc, rows] = (e[0] + e[1]) + (e[2] + e[3])
            return carry

        lax.fori_loop(0, 1024 // EXP_ROWS, block, 0)

    def logits_copy(j):
        return remote(lg_send.at[j], lg_all.at[head], lg_out.at[j], lg_sem.at[head], (ctx, j))

    def send_logits(par):
        for xx in range(4):
            j = par * 4 + xx
            for yy in range(4):
                a = logits[par * 8 + xx, :, 64 * yy:64 * yy + 64]
                b = logits[par * 8 + 4 + yy, :, 64 * xx:64 * xx + 64]
                lg_send[j, :, 128 * yy:128 * yy + 128] = jnp.concatenate([a, b], axis=1)

            @pl.when(j != head)
            def _():
                logits_copy(j).start()

            @pl.when(j == head)
            def _():
                lg_all[head] = lg_send[j]

    def turn_of(i):
        par_rel = jnp.where((i == 2) | (i >= 5), 1, 0)
        du = jnp.where(i < 2, i, jnp.where(i < 5, lax.rem(6 - i, 4), jnp.where(i == 5, 1, 9 - i)))
        return par_rel, du, zl + par_rel * (1 - 2 * zl)

    def recv_col(par, du):
        recv(keys.at[par, 0, pl.ds(0, 3), pl.ds(0, 2)], col_sem.at[par, lax.rem(pu + du, 4)])

    def arrivals(par_rel, du):
        @pl.when(par_rel == 0)
        def _():
            recv_col(zl, du)
            pl.when(du == 1)(lambda: by_core(lambda which: start_all(turn_along_z(which, 1))))

        @pl.when((par_rel == 1) & (du < 2))
        def _():
            for g in range(2):
                recv(keys.at[other, 0, :, pl.ds(0, 1)], turn_sem.at[other, lax.rem(pu + du, 4), g])

        @pl.when((par_rel == 1) & (du >= 2))
        def _():
            recv_col(other, du)

        by_core(lambda which: turn_to_twin(which, par_rel, du).start())

    def step(i, carry):
        par_rel, du, par = turn_of(i)
        pair = lax.div(du, 2)
        second = jnp.where(pair == 1, 3 - du, du)
        w_mine = lax.rem(pair_base(core) + du, 4)
        w_twin = lax.rem(pair_base(twin_half) + du, 4)

        held = par_rel * 4 + second
        next_rel, next_du, _ = turn_of(i + 1)

        @pl.when(i == 0)
        def _():
            recv(keys.at[par, 0, pl.ds(0, 3), pl.ds(0, 2)], twin_in.at[par, w_twin])

        @pl.when(i > 0)
        def _():
            recv(keys.at[par, 0, :, pl.ds(0, 2)], twin_in.at[par, w_twin])

        @pl.when((i >= 1) & (i < 7))
        def _():
            arrivals(next_rel, next_du)

        assemble(0, par, core, w_mine)
        assemble(1, par, twin_half, w_twin)
        chunk(0, held + 2 * core, par, core, w_mine)
        chunk(1, held + 2 * twin_half, par, twin_half, w_twin)

        @pl.when(i == 0)
        def _():
            for eu in (3, 2):
                for g in range(2):
                    recv(part(other, pu + eu, pv, g, 1), row_sem.at[other, lax.rem(pu + eu, 4), 1 + g])
                start_all(along_v(1, eu))

        @pl.when(i < 1)
        def _():
            arrivals(next_rel, next_du)

        @pl.when((i == 1) | (i == 4) | (i == 5) | (i == 7))
        def _():
            exponentials(par_rel * 4, par, 0, pair)
            exponentials(par_rel * 4, par, 1, pair)

        @pl.when((i == 4) | (i == 7))
        def _():
            send_logits(par)

        return carry

    recv_col(zl, 0)
    by_core(lambda which: start_all(turn_along_z(which, 0)))
    for dv in (1, 3, 2):
        first_to_twin(dv).start()
    lax.fori_loop(0, 8, step, 0)

    def normalise(rb, carry):
        rows = pl.ds(pl.multiple_of(rb * 256, 256), 256)
        m = [peaks[s, rows] for s in range(8)]
        top = jnp.max(functools.reduce(jnp.maximum, m), axis=1, keepdims=True)
        w = [jnp.exp2((v - top) * EXP_SCALE) for v in m]
        total = functools.reduce(jnp.add, [sums[s, rows] * w[s] for s in range(8)])
        share = 1.0 / (jnp.sum(total, axis=1, keepdims=True) * TEACHER_HEADS)
        for s in range(8):
            wts[s, rows] = w[s] * share
        return carry

    lax.fori_loop(0, 4, normalise, 0)

    def weigh(cp, d):
        parts = []
        for o in range(2):
            ci = cp * 2 + o
            sch = ci // 4
            half = sch % 2
            sc = sch * 2 + ((ci % 4 - pair_base(half) + 4) % 4) // 2
            acc = None
            for j in range(16):
                rows = pl.ds(pl.multiple_of(j * 64 + d * 8, 8), 8)
                wt = wts[sc, rows]
                term = expo[ci, rows] * jnp.concatenate([wt, wt], axis=1)
                acc = term if acc is None else acc + term
            parts.append(acc)
        return jnp.concatenate(parts, axis=0)

    for r in (1, 3, 2, 0):
        zi = (zh + r) % 4

        def to_twin(cp, carry):
            p_twin[zi, pl.ds(pl.multiple_of(cp * 16, 16), 16)] = weigh(cp, zi * 2 + 1 - core).astype(BF16)
            return carry

        unrolled(8, 4, to_twin, 0)
        send(p_twin.at[zi], p_twin_in.at[zi], twin_sem.at[zi], twin)

    for r in (1, 3, 2, 0):
        zi = (zh + r) % 4

        def mine(cp, carry):
            p_mine[cp] = weigh(cp, zi * 2 + core)
            return carry

        unrolled(8, 4, mine, 0)
        recv(p_twin_in.at[zi], twin_sem.at[zi])
        if r:

            def to_z(cp, carry):
                rows = pl.ds(pl.multiple_of(cp * 16, 16), 16)
                p_z[zi, rows] = (p_mine[cp] + p_twin_in[zi, rows].astype(F32)).astype(BF16)
                return carry

            unrolled(8, 4, to_z, 0)
            send(p_z.at[zi], p_z_in.at[zh], z_sem.at[zh], (ctx, zi * 2 + core))

    shape = (8, 256)
    pos8 = position(head * 8 + lax.broadcasted_iota(jnp.int32, shape, 0))
    masked = []
    for ci in range(16):
        seen = key_index(shape, ci // 8, (ci // 4) % 2, ci % 4) <= pos8
        masked.append(jnp.where(seen, logits[ci], NEG))
    top = jnp.max(functools.reduce(jnp.maximum, masked), axis=1, keepdims=True)
    total = functools.reduce(jnp.add, [jnp.exp(v - top) for v in masked])
    lse = top + jnp.log(jnp.sum(total, axis=1, keepdims=True))

    for r in (1, 3, 2):
        recv(p_z_in.at[(zh + r) % 4], z_sem.at[(zh + r) % 4])

    def finish(cp, carry):
        rows = pl.ds(pl.multiple_of(cp * 16, 16), 16)
        p = p_mine[cp] + p_twin_in[zh, rows].astype(F32)
        for r in (1, 3, 2):
            p = p + p_z_in[(zh + r) % 4, rows].astype(F32)
        lg = jnp.concatenate([logits[cp * 2], logits[cp * 2 + 1]], axis=0)
        term = p * (jnp.log(jnp.where(p > 0, p, 1.0)) - lg)
        mass, cross = carry
        return mass + p[0:8] + p[8:16], cross + term[0:8] + term[8:16]

    zero = jnp.zeros((8, 256), F32)
    mass, cross = lax.fori_loop(0, 8, finish, (zero, zero))
    mass = jnp.sum(mass, axis=1, keepdims=True)
    div = jnp.sum(cross, axis=1, keepdims=True) / mass - jnp.log(mass) + lse
    div_all[head] = jnp.broadcast_to(div, (8, 128))
    for dev in mates:
        send(div_all.at[head], div_all.at[head], div_sem.at[head], dev)

    for r in range(1, 8):
        d = (head + r) % 8
        recv(lg_all.at[d], lg_sem.at[d])
    for d in range(8):
        out_ref[8 * d:8 * d + 8, :] = lg_all[d]
    for r in range(1, 8):
        d = (head + r) % 8
        recv(div_all.at[d], div_sem.at[d])
    column = jnp.concatenate([div_all[d] for d in range(8)] + [jnp.zeros((64, 128), F32)], axis=0)
    div_ref[...] = column.T[0:8]
    for copy in sends:
        copy.wait_send()

    sent = [first_to_twin(dv) for dv in (1, 3, 2)]
    for du in range(4):
        sent += along_v(0, du) + (turn_along_z(0, du) if du < 2 else row_along_z(du) + along_v(1, du))
        sent += [turn_to_twin(0, 1, du)] + ([turn_to_twin(0, 0, du)] if du else [])
    for copy in sent:
        copy.wait_send()
    for r in range(1, 8):
        logits_copy(lax.rem(head + r, 8)).wait_send()


def hand_over(logits_ref, div_ref, out_ref, out_div_ref):
    out_ref[...] = logits_ref[...]
    out_div_ref[...] = div_ref[0:1, 0:64]


def local(teacher_queries, latent_keys, index_queries, index_keys, index_weights, block_start):
    vmem = pl.BlockSpec(memory_space=pltpu.VMEM)
    dma = pltpu.SemaphoreType.DMA
    logits, div = pl.pallas_call(
        kernel,
        out_shape=(jax.ShapeDtypeStruct((64, 512), F32), jax.ShapeDtypeStruct((8, 128), F32)),
        in_specs=[
            pl.BlockSpec(memory_space=pl.ANY), vmem, vmem, vmem, vmem,
            pl.BlockSpec(memory_space=pltpu.SMEM),
        ],
        out_specs=(vmem, vmem),
        scratch_shapes=[
            pltpu.VMEM((64, 9216), BF16),
            pltpu.VMEM((1024, 640), BF16),
            pltpu.VMEM((2, 4, 4, 4, 16, 1408), BF16),
            pltpu.VMEM((2, 256, 640), BF16),
            pltpu.VMEM((2, 256, 128), BF16),
            pltpu.VMEM((2, 640, 256), BF16),
            pltpu.VMEM((2, 128, 256), BF16),
            pltpu.VMEM((8, 1024, 256), F32),
            pltpu.VMEM((16, 1024, 256), F32),
            pltpu.VMEM((8, 1024, 128), F32),
            pltpu.VMEM((8, 1024, 128), F32),
            pltpu.VMEM((8, 1024, 128), F32),
            pltpu.VMEM((8, 64, 128), BF16),
            pltpu.VMEM((512, 128), BF16),
            pltpu.VMEM((64, 128), F32),
            pltpu.VMEM((8, 8, 128), F32),
            pltpu.VMEM((512, 128), F32),
            pltpu.VMEM((16, 8, 256), F32),
            pltpu.VMEM((8, 8, 512), F32),
            pltpu.VMEM((8, 8, 512), F32),
            pltpu.VMEM((8, 16, 256), F32),
            pltpu.VMEM((4, 128, 256), BF16),
            pltpu.VMEM((4, 128, 256), BF16),
            pltpu.VMEM((4, 128, 256), BF16),
            pltpu.VMEM((4, 128, 256), BF16),
            pltpu.VMEM((8, 8, 128), F32),
            dma(()), dma((32,)),
            dma((8,)), dma((4,)), dma((8, 4)), dma((4, 2)), dma((2, 2)), dma((8,)),
            dma((2, 4, 3)), dma((2, 4)), dma((2, 4, 2)), dma((2, 4)),
            dma((8,)), dma((8,)), dma((8,)), dma((4,)), dma((4,)), dma((8,)),
        ],
        compiler_params=pltpu.CompilerParams(
            collective_id=0, has_side_effects=True, vmem_limit_bytes=56 << 20
        ),
    )(teacher_queries, latent_keys.T, index_queries, index_keys, index_weights.T, block_start)
    logits, div = pl.pallas_call(
        hand_over,
        out_shape=(jax.ShapeDtypeStruct((64, 512), F32), jax.ShapeDtypeStruct((1, 64), F32)),
        in_specs=[vmem, vmem],
        out_specs=(vmem, vmem),
    )(logits, div)
    return logits, div.reshape(64)


def solution(mesh):
    return jax.shard_map(
        local,
        mesh=mesh,
        in_specs=(
            P("ctx", "head"),
            P("ctx", None),
            P("ctx", "head"),
            P("ctx", None),
            P("ctx", "head"),
            P("ctx"),
        ),
        out_specs=(P("ctx", "head"), P("ctx")),
        check_vma=False,
    )
```

```python
import functools

import jax
import jax.numpy as jnp
from jax import lax
from jax.experimental import pallas as pl
from jax.experimental.pallas import tpu as pltpu
from jax.sharding import PartitionSpec as P

MESH = pl.DeviceIdType.MESH
F32, BF16 = jnp.float32, jnp.bfloat16
TEACHER_HEADS = 128
LATENT, ROPE, WIDTH, IDIM = 512, 64, 576, 128
NEG = -1e30
EXP_ROWS = 512
EXP_SCALE = 192.0 ** (-0.5) * 1.4426950408889634
INDEX_SCALE = 128.0 ** (-0.5)
ORDER = (0, 1, 3, 2)


def unrolled(n, by, body, carry):
    def several(i, carry):
        for u in range(by):
            carry = body(i * by + u, carry)
        return carry

    return lax.fori_loop(0, n // by, several, carry)


def kernel(
    tq_hbm, lk_ref, iq_ref, ik_ref, iw_ref, bs_ref,
    out_ref, div_ref,
    tq, q_rows, keys, kc, ki, kct, kit, raw, expo, peaks, sums, wts,
    iq_send, iq_all, iw_send, iw_recv, iw_all, logits, lg_send, lg_all,
    p_mine, p_twin, p_twin_in, p_z, p_z_in, div_all,
    copy_sem, send_sem, twin_out, first_out, v_out, row_out, turn_out, lg_out, row_sem, col_sem, turn_sem, twin_in, iq_sem, iw_sem, lg_sem, twin_sem, z_sem, div_sem,
):
    ctx, head = lax.axis_index("ctx"), lax.axis_index("head")
    zl, x, y = ctx // 16, (ctx // 4) % 4, ctx % 4
    zh, core = head // 2, head % 2
    z = zh * 2 + zl
    pu, pv = x + core * (y - x), y + core * (x - y)
    twin = (ctx, zh * 2 + 1 - core)

    def ctx_of(par, u, v):
        u, v = lax.rem(u, 4), lax.rem(v, 4)
        return par * 16 + (u + core * (v - u)) * 4 + v + core * (u - v)

    def z_device(dz):
        zz = (z + dz + 8) % 8
        return ((zz % 2) * 16 + x * 4 + y, (zz // 2) * 2 + core)

    u_devs = {d: (ctx_of(zl, pu + d, pv), head) for d in (1, 3, 2)}
    v_devs = {d: (ctx_of(zl, pu, pv + d), head) for d in (1, 3, 2)}
    first_dev = z_device(2 * core - 1)
    last_dev = z_device(1 - 2 * core)
    mates = [(ctx, (head + r) % 8) for r in range(1, 8)]

    tq_copy = pltpu.make_async_copy(tq_hbm, tq, copy_sem)
    tq_copy.start()

    barrier = pltpu.get_barrier_semaphore()
    partners = list(u_devs.values()) + list(v_devs.values()) + [first_dev, last_dev] + mates
    for dev in partners:
        pl.semaphore_signal(barrier, inc=1, device_id=dev, device_id_type=MESH)

    lat = [lk_ref[128 * t:128 * t + 128, :].T for t in range(4)]
    rope = jnp.concatenate([lk_ref[512:576, :].astype(F32), jnp.zeros((64, 128), F32)], axis=0).T
    for g in range(4):
        a, b = g * 32, g * 32 + 16
        for t in range(4):
            keys[zl, x, y, g, :, 128 * t:128 * t + 128] = lat[t][a:a + 16]
            keys[zl, x, y, g, :, 640 + 128 * t:768 + 128 * t] = lat[t][b:b + 16]
        keys[zl, x, y, g, :, 512:640] = ik_ref[a:a + 16, :]
        keys[zl, x, y, g, :, 1152:1280] = ik_ref[b:b + 16, :]
        keys[zl, x, y, g, :, 1280:1408] = (rope[a:a + 16] + pltpu.roll(rope[b:b + 16], 64, 1)).astype(BF16)

    pl.semaphore_wait(barrier, len(partners))

    sends = []

    def remote(src, dst, out_sem, in_sem, dev):
        return pltpu.make_async_remote_copy(
            src_ref=src, dst_ref=dst, send_sem=out_sem, recv_sem=in_sem,
            device_id=dev, device_id_type=MESH,
        )

    def send(src, dst, in_sem, dev):
        copy = remote(src, dst, send_sem.at[len(sends)], in_sem, dev)
        copy.start()
        sends.append(copy)

    def recv(dst, in_sem):
        remote(dst, dst, send_sem.at[0], in_sem, twin).wait_recv()

    def copies(ref, out_sem, in_sem, dev):
        return remote(ref, ref, out_sem, in_sem, dev)

    def part(par, u, v, group=0, n=2):
        u, v = lax.rem(u, 4), lax.rem(v, 4)
        return keys.at[par, u + core * (v - u), v + core * (u - v), pl.ds(g0 + group, n)]

    def turn_part(which, par, u, group, n):
        u = lax.rem(u, 4)
        if which == 0:
            return keys.at[par, u, :, pl.ds(g0 + group, n)]
        return keys.at[par, :, u, pl.ds(g0 + group, n)]

    def by_core(start):
        for which in range(2):
            pl.when(core == which)(functools.partial(start, which))

    def along_v(par_rel, du):
        par = zl + par_rel * (1 - 2 * zl)
        return [
            copies(part(par, pu + du, pv), v_out.at[par_rel * 4 + du, dv],
                   col_sem.at[par, lax.rem(pu + du, 4)], v_devs[dv])
            for dv in (1, 3, 2)
        ]

    def row_along_z(du):
        return [
            copies(part(zl, pu + du, pv, g, 1), row_out.at[du, g],
                   row_sem.at[zl, lax.rem(pu + du, 4), 1 + g], dev)
            for g, dev in ((0, last_dev), (1, first_dev))
        ]

    def turn_along_z(which, du):
        return [
            copies(turn_part(which, zl, pu + du, g, 1), turn_out.at[du, g],
                   turn_sem.at[zl, lax.rem(pu + du, 4), g], dev)
            for g, dev in ((0, last_dev), (1, first_dev))
        ]

    def turn_to_twin(which, par_rel, du):
        par = zl + par_rel * (1 - 2 * zl)
        return copies(turn_part(which, par, pu + du, 0, 2), twin_out.at[par_rel * 4 + du],
                      twin_in.at[par, lax.rem(pu + du, 4)], twin)

    def first_to_twin(dv):
        return copies(part(zl, pu, pv + dv), first_out.at[dv], twin_in.at[zl, pu], twin)

    def start_all(several):
        for copy in several:
            copy.start()

    near = lambda devs: [devs[1], devs[3], devs[2]]
    g0 = 2 * core
    other = 1 - zl
    twin_half = 1 - core
    for dev in near(u_devs):
        send(part(zl, pu, pv), part(zl, pu, pv), row_sem.at[zl, pu, 0], dev)

    iqf = iq_ref[...].astype(F32)
    for d in range(8):
        iq_send[d] = jnp.concatenate(
            [iqf[8 * d:8 * d + 8, 128 * j:128 * j + 128] for j in range(8)], axis=0
        ).astype(BF16)
    weights = jnp.concatenate([iw_ref[...].astype(F32), jnp.zeros((8, 64), F32)], axis=1)
    weights = jnp.concatenate([weights, jnp.zeros((120, 128), F32)], axis=0).T
    iw_send[...] = weights[0:64]

    for r, dev in enumerate(mates):
        d = (head + r + 1) % 8
        send(iq_send.at[d], iq_all.at[pl.ds(pl.multiple_of(head * 64, 64), 64)], iq_sem.at[head], dev)
        send(iw_send.at[pl.ds(pl.multiple_of(d * 8, 8), 8)], iw_recv.at[head], iw_sem.at[head], dev)

    tq_copy.wait()
    lane = lax.broadcasted_iota(jnp.int32, (64, 128), 1)

    def prepare(i, carry):
        base = pl.multiple_of(i * 1152, 128)
        row = pl.multiple_of(i * 128, 128)
        q_rows[pl.ds(row, 64), 0:512] = tq[:, pl.ds(base, 512)]
        tiles = [tq[:, pl.ds(base + 512 + 128 * t, 128)].astype(F32) for t in range(5)]
        q_rows[pl.ds(row, 64), 512:640] = jnp.where(lane < 64, tiles[0], 0.0).astype(BF16)
        rolled = [pltpu.roll(t, 64, 1) for t in tiles]
        rolled.append(jnp.zeros_like(rolled[0]))
        for t in range(5):
            q_rows[pl.ds(row + 64, 64), 128 * t:128 * t + 128] = jnp.where(
                lane < 64, rolled[t], rolled[t + 1]
            ).astype(BF16)
        return carry

    start_all(along_v(0, 0))
    lax.fori_loop(0, 8, prepare, 0)

    for du in (1, 3, 2):
        recv(part(zl, pu + du, pv), row_sem.at[zl, lax.rem(pu + du, 4), 0])
        if du != 1:
            start_all(row_along_z(du))
        if du == 1:
            start_all(along_v(0, du))

    iq_all[pl.ds(pl.multiple_of(head * 64, 64), 64)] = iq_send[head]
    iw_recv[head] = iw_send[pl.ds(pl.multiple_of(head * 8, 8), 8)]
    for r in range(1, 8):
        d = (head + r) % 8
        recv(iq_all.at[pl.ds(pl.multiple_of(d * 64, 64), 64)], iq_sem.at[d])
        recv(iw_recv.at[d], iw_sem.at[d])
    for s in range(8):
        tile = iw_recv[s]
        for j in range(8):
            r = (s * 8 + j) * 8
            iw_all[r:r + 8, :] = jnp.broadcast_to(tile[:, j:j + 1], (8, 128))

    start0, start1 = bs_ref[0], bs_ref[1]

    def position(q):
        return jnp.where(q < 32, start0, start1) + q % 32

    def key_index(shape, par, half, w):
        sw, sj = 4 - 3 * half, 1 + 3 * half
        col = lax.broadcasted_iota(jnp.int32, shape, 1)
        return (par * 16 + w * sw) * 128 + half * 64 + (col // 64) * (sj * 128) + col % 64

    def assemble(slot, par, half, w):
        for j in range(4):
            kx, ky = w + half * (j - w), j + half * (w - j)
            for g in range(2):
                r = j * 64 + g * 32
                packed = keys[par, kx, ky, 2 * half + g]
                kc[slot, r:r + 16, 0:512] = packed[:, 0:512]
                ki[slot, r:r + 16, :] = packed[:, 512:640]
                kc[slot, r + 16:r + 32, 0:512] = packed[:, 640:1152]
                ki[slot, r + 16:r + 32, :] = packed[:, 1152:1280]
                rope = packed[:, 1280:1408]
                kc[slot, r:r + 16, 512:640] = rope
                kc[slot, r + 16:r + 32, 512:640] = pltpu.roll(rope.astype(F32), 64, 1).astype(BF16)
        kct[slot] = kc[slot].T
        kit[slot] = ki[slot].T

    def chunk(slot, held, par, half, w):
        ci = par * 8 + half * 4 + w
        shape = (64, 256)
        seen = key_index(shape, par, half, w) <= position(lax.broadcasted_iota(jnp.int32, shape, 0))
        bias = jnp.where(seen, 0.0, NEG)
        scores = jnp.dot(q_rows[...], kct[slot], preferred_element_type=F32)
        raw[held] = (scores.reshape(16, 64, 256) + bias[None]).reshape(1024, 256)

        s = jnp.dot(iq_all[...], kit[slot], preferred_element_type=F32)
        wt = iw_all[...]
        s = jnp.maximum(s, 0.0) * jnp.concatenate([wt, wt], axis=1)
        lg = jnp.sum(s.reshape(64, 8, 256), axis=0) * INDEX_SCALE
        shape = (8, 256)
        seen = key_index(shape, par, half, w) <= position(
            head * 8 + lax.broadcasted_iota(jnp.int32, shape, 0)
        )
        logits[ci] = jnp.where(seen, lg, 0.0)

    def pair_base(half):
        return x + half * (y - x)

    def exponentials(held, par, half, pair):
        base = pair_base(half)
        ca = par * 8 + half * 4 + lax.rem(base + 3 * pair, 4)
        cb = par * 8 + half * 4 + lax.rem(base + 1 + pair, 4)
        sc = (par * 2 + half) * 2 + pair
        held = held + 2 * half

        def block(rb, carry):
            rows = pl.ds(pl.multiple_of(rb * EXP_ROWS, EXP_ROWS), EXP_ROWS)
            refs = [(0, ca, 0), (0, ca, 128), (1, cb, 0), (1, cb, 128)]
            t = [raw[held + o, rows, l:l + 128] for o, _, l in refs]
            peak = jnp.maximum(jnp.maximum(t[0], t[1]), jnp.maximum(t[2], t[3]))
            e = [jnp.exp2((v - peak) * EXP_SCALE) for v in t]
            for (_, c, l), v in zip(refs, e):
                expo[c, rows, l:l + 128] = v
            peaks[sc, rows] = peak
            sums[sc, rows] = (e[0] + e[1]) + (e[2] + e[3])
            return carry

        lax.fori_loop(0, 1024 // EXP_ROWS, block, 0)

    def logits_copy(j):
        return remote(lg_send.at[j], lg_all.at[head], lg_out.at[j], lg_sem.at[head], (ctx, j))

    def send_logits(par):
        for xx in range(4):
            j = par * 4 + xx
            for yy in range(4):
                a = logits[par * 8 + xx, :, 64 * yy:64 * yy + 64]
                b = logits[par * 8 + 4 + yy, :, 64 * xx:64 * xx + 64]
                lg_send[j, :, 128 * yy:128 * yy + 128] = jnp.concatenate([a, b], axis=1)

            @pl.when(j != head)
            def _():
                logits_copy(j).start()

            @pl.when(j == head)
            def _():
                lg_all[head] = lg_send[j]

    def turn_of(i):
        par_rel = jnp.where((i == 2) | (i >= 5), 1, 0)
        du = jnp.where(i < 2, i, jnp.where(i < 5, lax.rem(6 - i, 4), jnp.where(i == 5, 1, 9 - i)))
        return par_rel, du, zl + par_rel * (1 - 2 * zl)

    def recv_col(par, du):
        recv(keys.at[par, 0, pl.ds(0, 3), pl.ds(0, 2)], col_sem.at[par, lax.rem(pu + du, 4)])

    def arrivals(par_rel, du):
        @pl.when(par_rel == 0)
        def _():
            recv_col(zl, du)
            pl.when(du == 1)(lambda: by_core(lambda which: start_all(turn_along_z(which, 1))))

        @pl.when((par_rel == 1) & (du < 2))
        def _():
            for g in range(2):
                recv(keys.at[other, 0, :, pl.ds(0, 1)], turn_sem.at[other, lax.rem(pu + du, 4), g])

        @pl.when((par_rel == 1) & (du >= 2))
        def _():
            recv_col(other, du)

        by_core(lambda which: turn_to_twin(which, par_rel, du).start())

    def step(i, carry):
        par_rel, du, par = turn_of(i)
        pair = lax.div(du, 2)
        second = jnp.where(pair == 1, 3 - du, du)
        w_mine = lax.rem(pair_base(core) + du, 4)
        w_twin = lax.rem(pair_base(twin_half) + du, 4)

        held = par_rel * 4 + second
        next_rel, next_du, _ = turn_of(i + 1)

        @pl.when(i == 0)
        def _():
            recv(keys.at[par, 0, pl.ds(0, 3), pl.ds(0, 2)], twin_in.at[par, w_twin])

        @pl.when(i > 0)
        def _():
            recv(keys.at[par, 0, :, pl.ds(0, 2)], twin_in.at[par, w_twin])

        @pl.when((i >= 1) & (i < 7))
        def _():
            arrivals(next_rel, next_du)

        @pl.when(i == 0)
        def _():
            start_all(along_v(0, 3))

        assemble(0, par, core, w_mine)
        assemble(1, par, twin_half, w_twin)
        chunk(0, held + 2 * core, par, core, w_mine)
        chunk(1, held + 2 * twin_half, par, twin_half, w_twin)

        @pl.when(i == 0)
        def _():
            start_all(along_v(0, 2))
            for eu in (3, 2):
                for g in range(2):
                    recv(part(other, pu + eu, pv, g, 1), row_sem.at[other, lax.rem(pu + eu, 4), 1 + g])
                start_all(along_v(1, eu))

        @pl.when(i < 1)
        def _():
            arrivals(next_rel, next_du)

        @pl.when((i == 1) | (i == 4) | (i == 5) | (i == 7))
        def _():
            exponentials(par_rel * 4, par, 0, pair)
            exponentials(par_rel * 4, par, 1, pair)

        @pl.when((i == 4) | (i == 7))
        def _():
            send_logits(par)

        return carry

    recv_col(zl, 0)
    by_core(lambda which: start_all(turn_along_z(which, 0)))
    for dv in (1, 3, 2):
        first_to_twin(dv).start()
    lax.fori_loop(0, 8, step, 0)

    def normalise(rb, carry):
        rows = pl.ds(pl.multiple_of(rb * 256, 256), 256)
        m = [peaks[s, rows] for s in range(8)]
        top = jnp.max(functools.reduce(jnp.maximum, m), axis=1, keepdims=True)
        w = [jnp.exp2((v - top) * EXP_SCALE) for v in m]
        total = functools.reduce(jnp.add, [sums[s, rows] * w[s] for s in range(8)])
        share = 1.0 / (jnp.sum(total, axis=1, keepdims=True) * TEACHER_HEADS)
        for s in range(8):
            wts[s, rows] = w[s] * share
        return carry

    lax.fori_loop(0, 4, normalise, 0)

    def weigh(cp, d):
        parts = []
        for o in range(2):
            ci = cp * 2 + o
            sch = ci // 4
            half = sch % 2
            sc = sch * 2 + ((ci % 4 - pair_base(half) + 4) % 4) // 2
            acc = None
            for j in range(16):
                rows = pl.ds(pl.multiple_of(j * 64 + d * 8, 8), 8)
                wt = wts[sc, rows]
                term = expo[ci, rows] * jnp.concatenate([wt, wt], axis=1)
                acc = term if acc is None else acc + term
            parts.append(acc)
        return jnp.concatenate(parts, axis=0)

    for r in (2, 1, 3, 0):
        zi = (zh + r) % 4

        def to_twin(cp, carry):
            p_twin[zi, pl.ds(pl.multiple_of(cp * 16, 16), 16)] = weigh(cp, zi * 2 + 1 - core).astype(BF16)
            return carry

        unrolled(8, 4, to_twin, 0)
        send(p_twin.at[zi], p_twin_in.at[zi], twin_sem.at[zi], twin)

    for r in (2, 1, 3, 0):
        zi = (zh + r) % 4

        recv(p_twin_in.at[zi], twin_sem.at[zi])

        def mine(cp, carry):
            rows = pl.ds(pl.multiple_of(cp * 16, 16), 16)
            p = weigh(cp, zi * 2 + core) + p_twin_in[zi, rows].astype(F32)
            if r:
                p_z[zi, rows] = p.astype(BF16)
            else:
                p_mine[cp] = p
            return carry

        unrolled(8, 4, mine, 0)
        if r:
            send(p_z.at[zi], p_z_in.at[zh], z_sem.at[zh], (ctx, zi * 2 + core))

    shape = (8, 256)
    pos8 = position(head * 8 + lax.broadcasted_iota(jnp.int32, shape, 0))
    masked = []
    for ci in range(16):
        seen = key_index(shape, ci // 8, (ci // 4) % 2, ci % 4) <= pos8
        masked.append(jnp.where(seen, logits[ci], NEG))
    top = jnp.max(functools.reduce(jnp.maximum, masked), axis=1, keepdims=True)
    total = functools.reduce(jnp.add, [jnp.exp(v - top) for v in masked])
    lse = top + jnp.log(jnp.sum(total, axis=1, keepdims=True))

    for r in (1, 3, 2):
        recv(p_z_in.at[(zh + r) % 4], z_sem.at[(zh + r) % 4])

    def finish(cp, carry):
        rows = pl.ds(pl.multiple_of(cp * 16, 16), 16)
        p = p_mine[cp]
        for r in (1, 3, 2):
            p = p + p_z_in[(zh + r) % 4, rows].astype(F32)
        lg = jnp.concatenate([logits[cp * 2], logits[cp * 2 + 1]], axis=0)
        term = p * (jnp.log(jnp.where(p > 0, p, 1.0)) - lg)
        mass, cross = carry
        return mass + p[0:8] + p[8:16], cross + term[0:8] + term[8:16]

    zero = jnp.zeros((8, 256), F32)
    mass, cross = unrolled(8, 4, finish, (zero, zero))
    mass = jnp.sum(mass, axis=1, keepdims=True)
    div = jnp.sum(cross, axis=1, keepdims=True) / mass - jnp.log(mass) + lse
    div_all[head] = jnp.broadcast_to(div, (8, 128))
    for dev in mates:
        send(div_all.at[head], div_all.at[head], div_sem.at[head], dev)

    for r in range(1, 8):
        d = (head + r) % 8
        recv(lg_all.at[d], lg_sem.at[d])
    for d in range(8):
        out_ref[8 * d:8 * d + 8, :] = lg_all[d]
    for copy in sends[:-7]:
        copy.wait_send()

    sent = [first_to_twin(dv) for dv in (1, 3, 2)]
    for du in range(4):
        sent += along_v(0, du) + (turn_along_z(0, du) if du < 2 else row_along_z(du) + along_v(1, du))
        sent += [turn_to_twin(0, 1, du)] + ([turn_to_twin(0, 0, du)] if du else [])
    for copy in sent:
        copy.wait_send()
    for r in range(1, 8):
        logits_copy(lax.rem(head + r, 8)).wait_send()

    for r in range(1, 8):
        d = (head + r) % 8
        recv(div_all.at[d], div_sem.at[d])
    column = jnp.concatenate([div_all[d] for d in range(8)] + [jnp.zeros((64, 128), F32)], axis=0)
    div_ref[...] = column.T[0:8]

    for copy in sends[-7:]:
        copy.wait_send()


def hand_over(logits_ref, div_ref, out_ref, out_div_ref):
    out_ref[...] = logits_ref[...]
    out_div_ref[...] = div_ref[0:1, 0:64]


def local(teacher_queries, latent_keys, index_queries, index_keys, index_weights, block_start):
    vmem = pl.BlockSpec(memory_space=pltpu.VMEM)
    dma = pltpu.SemaphoreType.DMA
    logits, div = pl.pallas_call(
        kernel,
        out_shape=(jax.ShapeDtypeStruct((64, 512), F32), jax.ShapeDtypeStruct((8, 128), F32)),
        in_specs=[
            pl.BlockSpec(memory_space=pl.ANY), vmem, vmem, vmem, vmem,
            pl.BlockSpec(memory_space=pltpu.SMEM),
        ],
        out_specs=(vmem, vmem),
        scratch_shapes=[
            pltpu.VMEM((64, 9216), BF16),
            pltpu.VMEM((1024, 640), BF16),
            pltpu.VMEM((2, 4, 4, 4, 16, 1408), BF16),
            pltpu.VMEM((2, 256, 640), BF16),
            pltpu.VMEM((2, 256, 128), BF16),
            pltpu.VMEM((2, 640, 256), BF16),
            pltpu.VMEM((2, 128, 256), BF16),
            pltpu.VMEM((8, 1024, 256), F32),
            pltpu.VMEM((16, 1024, 256), F32),
            pltpu.VMEM((8, 1024, 128), F32),
            pltpu.VMEM((8, 1024, 128), F32),
            pltpu.VMEM((8, 1024, 128), F32),
            pltpu.VMEM((8, 64, 128), BF16),
            pltpu.VMEM((512, 128), BF16),
            pltpu.VMEM((64, 128), F32),
            pltpu.VMEM((8, 8, 128), F32),
            pltpu.VMEM((512, 128), F32),
            pltpu.VMEM((16, 8, 256), F32),
            pltpu.VMEM((8, 8, 512), F32),
            pltpu.VMEM((8, 8, 512), F32),
            pltpu.VMEM((8, 16, 256), F32),
            pltpu.VMEM((4, 128, 256), BF16),
            pltpu.VMEM((4, 128, 256), BF16),
            pltpu.VMEM((4, 128, 256), BF16),
            pltpu.VMEM((4, 128, 256), BF16),
            pltpu.VMEM((8, 8, 128), F32),
            dma(()), dma((32,)),
            dma((8,)), dma((4,)), dma((8, 4)), dma((4, 2)), dma((2, 2)), dma((8,)),
            dma((2, 4, 3)), dma((2, 4)), dma((2, 4, 2)), dma((2, 4)),
            dma((8,)), dma((8,)), dma((8,)), dma((4,)), dma((4,)), dma((8,)),
        ],
        compiler_params=pltpu.CompilerParams(
            collective_id=0, has_side_effects=True, vmem_limit_bytes=56 << 20
        ),
    )(teacher_queries, latent_keys.T, index_queries, index_keys, index_weights.T, block_start)
    logits, div = pl.pallas_call(
        hand_over,
        out_shape=(jax.ShapeDtypeStruct((64, 512), F32), jax.ShapeDtypeStruct((1, 64), F32)),
        in_specs=[vmem, vmem],
        out_specs=(vmem, vmem),
    )(logits, div)
    return logits, div.reshape(64)


def solution(mesh):
    return jax.shard_map(
        local,
        mesh=mesh,
        in_specs=(
            P("ctx", "head"),
            P("ctx", None),
            P("ctx", "head"),
            P("ctx", None),
            P("ctx", "head"),
            P("ctx"),
        ),
        out_specs=(P("ctx", "head"), P("ctx")),
        check_vma=False,
    )
```

```python
import functools

import jax
import jax.numpy as jnp
from jax import lax
from jax.experimental import pallas as pl
from jax.experimental.pallas import tpu as pltpu
from jax.sharding import PartitionSpec as P

MESH = pl.DeviceIdType.MESH
F32, BF16 = jnp.float32, jnp.bfloat16
TEACHER_HEADS = 128
LATENT, ROPE, WIDTH, IDIM = 512, 64, 576, 128
NEG = -1e30
EXP_ROWS = 512
EXP_SCALE = 192.0 ** (-0.5) * 1.4426950408889634
INDEX_SCALE = 128.0 ** (-0.5)
ORDER = (0, 1, 3, 2)


def unrolled(n, by, body, carry):
    def several(i, carry):
        for u in range(by):
            carry = body(i * by + u, carry)
        return carry

    return lax.fori_loop(0, n // by, several, carry)


def kernel(
    tq_hbm, lk_ref, iq_ref, ik_ref, iw_ref, bs_ref,
    out_ref, div_ref,
    tq, q_rows, keys, kc, ki, kct, kit, raw, expo, peaks, sums, wts,
    iq_send, iq_all, iw_send, iw_recv, iw_all, logits, lg_send, lg_all,
    p_mine, p_twin, p_twin_in, p_z, p_z_in, div_all,
    copy_sem, send_sem, twin_out, first_out, v_out, row_out, turn_out, lg_out, row_sem, col_sem, turn_sem, twin_in, iq_sem, iw_sem, lg_sem, twin_sem, z_sem, div_sem,
):
    ctx, head = lax.axis_index("ctx"), lax.axis_index("head")
    zl, x, y = ctx // 16, (ctx // 4) % 4, ctx % 4
    zh, core = head // 2, head % 2
    z = zh * 2 + zl
    pu, pv = x + core * (y - x), y + core * (x - y)
    twin = (ctx, zh * 2 + 1 - core)

    def ctx_of(par, u, v):
        u, v = lax.rem(u, 4), lax.rem(v, 4)
        return par * 16 + (u + core * (v - u)) * 4 + v + core * (u - v)

    def z_device(dz):
        zz = (z + dz + 8) % 8
        return ((zz % 2) * 16 + x * 4 + y, (zz // 2) * 2 + core)

    u_devs = {d: (ctx_of(zl, pu + d, pv), head) for d in (1, 3, 2)}
    v_devs = {d: (ctx_of(zl, pu, pv + d), head) for d in (1, 3, 2)}
    first_dev = z_device(2 * core - 1)
    last_dev = z_device(1 - 2 * core)
    mates = [(ctx, (head + r) % 8) for r in range(1, 8)]

    tq_copy = pltpu.make_async_copy(tq_hbm, tq, copy_sem)
    tq_copy.start()

    barrier = pltpu.get_barrier_semaphore()
    partners = list(u_devs.values()) + list(v_devs.values()) + [first_dev, last_dev] + mates
    for dev in partners:
        pl.semaphore_signal(barrier, inc=1, device_id=dev, device_id_type=MESH)

    lat = [lk_ref[128 * t:128 * t + 128, :].T for t in range(4)]
    rope = jnp.concatenate([lk_ref[512:576, :].astype(F32), jnp.zeros((64, 128), F32)], axis=0).T
    for g in range(4):
        a, b = g * 32, g * 32 + 16
        for t in range(4):
            keys[zl, x, y, g, :, 128 * t:128 * t + 128] = lat[t][a:a + 16]
            keys[zl, x, y, g, :, 640 + 128 * t:768 + 128 * t] = lat[t][b:b + 16]
        keys[zl, x, y, g, :, 512:640] = ik_ref[a:a + 16, :]
        keys[zl, x, y, g, :, 1152:1280] = ik_ref[b:b + 16, :]
        keys[zl, x, y, g, :, 1280:1408] = (rope[a:a + 16] + pltpu.roll(rope[b:b + 16], 64, 1)).astype(BF16)

    pl.semaphore_wait(barrier, len(partners))

    sends = []

    def remote(src, dst, out_sem, in_sem, dev):
        return pltpu.make_async_remote_copy(
            src_ref=src, dst_ref=dst, send_sem=out_sem, recv_sem=in_sem,
            device_id=dev, device_id_type=MESH,
        )

    def send(src, dst, in_sem, dev):
        copy = remote(src, dst, send_sem.at[len(sends)], in_sem, dev)
        copy.start()
        sends.append(copy)

    def recv(dst, in_sem):
        remote(dst, dst, send_sem.at[0], in_sem, twin).wait_recv()

    def copies(ref, out_sem, in_sem, dev):
        return remote(ref, ref, out_sem, in_sem, dev)

    def part(par, u, v, group=0, n=2):
        u, v = lax.rem(u, 4), lax.rem(v, 4)
        return keys.at[par, u + core * (v - u), v + core * (u - v), pl.ds(g0 + group, n)]

    def turn_part(which, par, u, group, n):
        u = lax.rem(u, 4)
        if which == 0:
            return keys.at[par, u, :, pl.ds(g0 + group, n)]
        return keys.at[par, :, u, pl.ds(g0 + group, n)]

    def by_core(start):
        for which in range(2):
            pl.when(core == which)(functools.partial(start, which))

    def along_v(par_rel, du):
        par = zl + par_rel * (1 - 2 * zl)
        return [
            copies(part(par, pu + du, pv), v_out.at[par_rel * 4 + du, dv],
                   col_sem.at[par, lax.rem(pu + du, 4)], v_devs[dv])
            for dv in (1, 3, 2)
        ]

    def row_along_z(du):
        return [
            copies(part(zl, pu + du, pv, g, 1), row_out.at[du, g],
                   row_sem.at[zl, lax.rem(pu + du, 4), 1 + g], dev)
            for g, dev in ((0, last_dev), (1, first_dev))
        ]

    def turn_along_z(which, du):
        return [
            copies(turn_part(which, zl, pu + du, g, 1), turn_out.at[du, g],
                   turn_sem.at[zl, lax.rem(pu + du, 4), g], dev)
            for g, dev in ((0, last_dev), (1, first_dev))
        ]

    def turn_to_twin(which, par_rel, du):
        par = zl + par_rel * (1 - 2 * zl)
        return copies(turn_part(which, par, pu + du, 0, 2), twin_out.at[par_rel * 4 + du],
                      twin_in.at[par, lax.rem(pu + du, 4)], twin)

    def first_to_twin(dv):
        return copies(part(zl, pu, pv + dv), first_out.at[dv], twin_in.at[zl, pu], twin)

    def start_all(several):
        for copy in several:
            copy.start()

    near = lambda devs: [devs[1], devs[3], devs[2]]
    g0 = 2 * core
    other = 1 - zl
    twin_half = 1 - core
    for dev in near(u_devs):
        send(part(zl, pu, pv), part(zl, pu, pv), row_sem.at[zl, pu, 0], dev)

    iqf = iq_ref[...].astype(F32)
    for d in range(8):
        iq_send[d] = jnp.concatenate(
            [iqf[8 * d:8 * d + 8, 128 * j:128 * j + 128] for j in range(8)], axis=0
        ).astype(BF16)
    weights = jnp.concatenate([iw_ref[...].astype(F32), jnp.zeros((8, 64), F32)], axis=1)
    weights = jnp.concatenate([weights, jnp.zeros((120, 128), F32)], axis=0).T
    iw_send[...] = weights[0:64]

    for r, dev in enumerate(mates):
        d = (head + r + 1) % 8
        send(iq_send.at[d], iq_all.at[pl.ds(pl.multiple_of(head * 64, 64), 64)], iq_sem.at[head], dev)
        send(iw_send.at[pl.ds(pl.multiple_of(d * 8, 8), 8)], iw_recv.at[head], iw_sem.at[head], dev)

    tq_copy.wait()
    lane = lax.broadcasted_iota(jnp.int32, (64, 128), 1)

    def prepare(i, carry):
        base = pl.multiple_of(i * 1152, 128)
        row = pl.multiple_of(i * 128, 128)
        q_rows[pl.ds(row, 64), 0:512] = tq[:, pl.ds(base, 512)]
        tiles = [tq[:, pl.ds(base + 512 + 128 * t, 128)].astype(F32) for t in range(5)]
        q_rows[pl.ds(row, 64), 512:640] = jnp.where(lane < 64, tiles[0], 0.0).astype(BF16)
        rolled = [pltpu.roll(t, 64, 1) for t in tiles]
        rolled.append(jnp.zeros_like(rolled[0]))
        for t in range(5):
            q_rows[pl.ds(row + 64, 64), 128 * t:128 * t + 128] = jnp.where(
                lane < 64, rolled[t], rolled[t + 1]
            ).astype(BF16)
        return carry

    start_all(along_v(0, 0))
    lax.fori_loop(0, 8, prepare, 0)

    for du in (1, 3, 2):
        recv(part(zl, pu + du, pv), row_sem.at[zl, lax.rem(pu + du, 4), 0])
        if du != 1:
            start_all(row_along_z(du))
        if du == 1:
            start_all(along_v(0, du))

    iq_all[pl.ds(pl.multiple_of(head * 64, 64), 64)] = iq_send[head]
    iw_recv[head] = iw_send[pl.ds(pl.multiple_of(head * 8, 8), 8)]
    for r in range(1, 8):
        d = (head + r) % 8
        recv(iq_all.at[pl.ds(pl.multiple_of(d * 64, 64), 64)], iq_sem.at[d])
        recv(iw_recv.at[d], iw_sem.at[d])
    for s in range(8):
        tile = iw_recv[s]
        for j in range(8):
            r = (s * 8 + j) * 8
            iw_all[r:r + 8, :] = jnp.broadcast_to(tile[:, j:j + 1], (8, 128))

    start0, start1 = bs_ref[0], bs_ref[1]

    def position(q):
        return jnp.where(q < 32, start0, start1) + q % 32

    def key_index(shape, par, half, w):
        sw, sj = 4 - 3 * half, 1 + 3 * half
        col = lax.broadcasted_iota(jnp.int32, shape, 1)
        return (par * 16 + w * sw) * 128 + half * 64 + (col // 64) * (sj * 128) + col % 64

    def assemble(slot, par, half, w):
        for j in range(4):
            kx, ky = w + half * (j - w), j + half * (w - j)
            for g in range(2):
                r = j * 64 + g * 32
                packed = keys[par, kx, ky, 2 * half + g]
                kc[slot, r:r + 16, 0:512] = packed[:, 0:512]
                ki[slot, r:r + 16, :] = packed[:, 512:640]
                kc[slot, r + 16:r + 32, 0:512] = packed[:, 640:1152]
                ki[slot, r + 16:r + 32, :] = packed[:, 1152:1280]
                rope = packed[:, 1280:1408]
                kc[slot, r:r + 16, 512:640] = rope
                kc[slot, r + 16:r + 32, 512:640] = pltpu.roll(rope.astype(F32), 64, 1).astype(BF16)
        kct[slot] = kc[slot].T
        kit[slot] = ki[slot].T

    def chunk(slot, held, par, half, w):
        ci = par * 8 + half * 4 + w
        shape = (64, 256)
        seen = key_index(shape, par, half, w) <= position(lax.broadcasted_iota(jnp.int32, shape, 0))
        bias = jnp.where(seen, 0.0, NEG)
        scores = jnp.dot(q_rows[...], kct[slot], preferred_element_type=F32)
        raw[held] = (scores.reshape(16, 64, 256) + bias[None]).reshape(1024, 256)

        s = jnp.dot(iq_all[...], kit[slot], preferred_element_type=F32)
        wt = iw_all[...]
        s = jnp.maximum(s, 0.0) * jnp.concatenate([wt, wt], axis=1)
        lg = jnp.sum(s.reshape(64, 8, 256), axis=0) * INDEX_SCALE
        shape = (8, 256)
        seen = key_index(shape, par, half, w) <= position(
            head * 8 + lax.broadcasted_iota(jnp.int32, shape, 0)
        )
        logits[ci] = jnp.where(seen, lg, 0.0)

    def pair_base(half):
        return x + half * (y - x)

    def exponentials(held, par, half, pair):
        base = pair_base(half)
        ca = par * 8 + half * 4 + lax.rem(base + 3 * pair, 4)
        cb = par * 8 + half * 4 + lax.rem(base + 1 + pair, 4)
        sc = (par * 2 + half) * 2 + pair
        held = held + 2 * half

        def block(rb, carry):
            rows = pl.ds(pl.multiple_of(rb * EXP_ROWS, EXP_ROWS), EXP_ROWS)
            refs = [(0, ca, 0), (0, ca, 128), (1, cb, 0), (1, cb, 128)]
            t = [raw[held + o, rows, l:l + 128] for o, _, l in refs]
            peak = jnp.maximum(jnp.maximum(t[0], t[1]), jnp.maximum(t[2], t[3]))
            e = [jnp.exp2((v - peak) * EXP_SCALE) for v in t]
            for (_, c, l), v in zip(refs, e):
                expo[c, rows, l:l + 128] = v
            peaks[sc, rows] = peak
            sums[sc, rows] = (e[0] + e[1]) + (e[2] + e[3])
            return carry

        lax.fori_loop(0, 1024 // EXP_ROWS, block, 0)

    def logits_copy(j):
        return remote(lg_send.at[j], lg_all.at[head], lg_out.at[j], lg_sem.at[head], (ctx, j))

    def send_logits(par):
        for xx in range(4):
            j = par * 4 + xx
            for yy in range(4):
                a = logits[par * 8 + xx, :, 64 * yy:64 * yy + 64]
                b = logits[par * 8 + 4 + yy, :, 64 * xx:64 * xx + 64]
                lg_send[j, :, 128 * yy:128 * yy + 128] = jnp.concatenate([a, b], axis=1)

            @pl.when(j != head)
            def _():
                logits_copy(j).start()

            @pl.when(j == head)
            def _():
                lg_all[head] = lg_send[j]

    def turn_of(i):
        par_rel = jnp.where((i == 2) | (i >= 5), 1, 0)
        du = jnp.where(i < 2, i, jnp.where(i < 5, lax.rem(6 - i, 4), jnp.where(i == 5, 1, 9 - i)))
        return par_rel, du, zl + par_rel * (1 - 2 * zl)

    def recv_col(par, du):
        recv(keys.at[par, 0, pl.ds(0, 3), pl.ds(0, 2)], col_sem.at[par, lax.rem(pu + du, 4)])

    def arrivals(par_rel, du):
        @pl.when(par_rel == 0)
        def _():
            recv_col(zl, du)
            pl.when(du == 1)(lambda: by_core(lambda which: start_all(turn_along_z(which, 1))))

        @pl.when((par_rel == 1) & (du < 2))
        def _():
            for g in range(2):
                recv(keys.at[other, 0, :, pl.ds(0, 1)], turn_sem.at[other, lax.rem(pu + du, 4), g])

        @pl.when((par_rel == 1) & (du >= 2))
        def _():
            recv_col(other, du)

        by_core(lambda which: turn_to_twin(which, par_rel, du).start())

    def step(i, carry):
        par_rel, du, par = turn_of(i)
        pair = lax.div(du, 2)
        second = jnp.where(pair == 1, 3 - du, du)
        w_mine = lax.rem(pair_base(core) + du, 4)
        w_twin = lax.rem(pair_base(twin_half) + du, 4)

        held = par_rel * 4 + second
        next_rel, next_du, _ = turn_of(i + 1)

        @pl.when(i == 0)
        def _():
            recv(keys.at[par, 0, pl.ds(0, 3), pl.ds(0, 2)], twin_in.at[par, w_twin])

        @pl.when(i > 0)
        def _():
            recv(keys.at[par, 0, :, pl.ds(0, 2)], twin_in.at[par, w_twin])

        @pl.when((i >= 1) & (i < 7))
        def _():
            arrivals(next_rel, next_du)

        @pl.when(i == 0)
        def _():
            start_all(along_v(0, 3))

        assemble(0, par, core, w_mine)
        assemble(1, par, twin_half, w_twin)
        chunk(0, held + 2 * core, par, core, w_mine)
        chunk(1, held + 2 * twin_half, par, twin_half, w_twin)

        @pl.when(i == 0)
        def _():
            start_all(along_v(0, 2))
            for eu in (3, 2):
                for g in range(2):
                    recv(part(other, pu + eu, pv, g, 1), row_sem.at[other, lax.rem(pu + eu, 4), 1 + g])
                start_all(along_v(1, eu))

        @pl.when(i < 1)
        def _():
            arrivals(next_rel, next_du)

        @pl.when((i == 1) | (i == 4) | (i == 5) | (i == 7))
        def _():
            exponentials(par_rel * 4, par, 0, pair)
            exponentials(par_rel * 4, par, 1, pair)

        @pl.when((i == 4) | (i == 7))
        def _():
            send_logits(par)

        return carry

    recv_col(zl, 0)
    by_core(lambda which: start_all(turn_along_z(which, 0)))
    for dv in (1, 3, 2):
        first_to_twin(dv).start()
    lax.fori_loop(0, 8, step, 0)

    def normalise(rb, carry):
        rows = pl.ds(pl.multiple_of(rb * 512, 512), 512)
        m = [peaks[s, rows] for s in range(8)]
        top = jnp.max(functools.reduce(jnp.maximum, m), axis=1, keepdims=True)
        w = [jnp.exp2((v - top) * EXP_SCALE) for v in m]
        total = functools.reduce(jnp.add, [sums[s, rows] * w[s] for s in range(8)])
        share = 1.0 / (jnp.sum(total, axis=1, keepdims=True) * TEACHER_HEADS)
        for s in range(8):
            wts[s, rows] = w[s] * share
        return carry

    lax.fori_loop(0, 2, normalise, 0)

    def weigh(cp, d):
        parts = []
        for o in range(2):
            ci = cp * 2 + o
            sch = ci // 4
            half = sch % 2
            sc = sch * 2 + ((ci % 4 - pair_base(half) + 4) % 4) // 2
            acc = None
            for j in range(16):
                rows = pl.ds(pl.multiple_of(j * 64 + d * 8, 8), 8)
                wt = wts[sc, rows]
                term = expo[ci, rows] * jnp.concatenate([wt, wt], axis=1)
                acc = term if acc is None else acc + term
            parts.append(acc)
        return jnp.concatenate(parts, axis=0)

    for r in (2, 1, 3, 0):
        zi = (zh + r) % 4

        def to_twin(cp, carry):
            p_twin[zi, pl.ds(pl.multiple_of(cp * 16, 16), 16)] = weigh(cp, zi * 2 + 1 - core).astype(BF16)
            return carry

        unrolled(8, 8, to_twin, 0)
        send(p_twin.at[zi], p_twin_in.at[zi], twin_sem.at[zi], twin)

    for r in (2, 1, 3, 0):
        zi = (zh + r) % 4

        recv(p_twin_in.at[zi], twin_sem.at[zi])

        def mine(cp, carry):
            rows = pl.ds(pl.multiple_of(cp * 16, 16), 16)
            p = weigh(cp, zi * 2 + core) + p_twin_in[zi, rows].astype(F32)
            if r:
                p_z[zi, rows] = p.astype(BF16)
            else:
                p_mine[cp] = p
            return carry

        unrolled(8, 8, mine, 0)
        if r:
            send(p_z.at[zi], p_z_in.at[zh], z_sem.at[zh], (ctx, zi * 2 + core))

    shape = (8, 256)
    pos8 = position(head * 8 + lax.broadcasted_iota(jnp.int32, shape, 0))
    masked = []
    for ci in range(16):
        seen = key_index(shape, ci // 8, (ci // 4) % 2, ci % 4) <= pos8
        masked.append(jnp.where(seen, logits[ci], NEG))
    top = jnp.max(functools.reduce(jnp.maximum, masked), axis=1, keepdims=True)
    total = functools.reduce(jnp.add, [jnp.exp(v - top) for v in masked])
    lse = top + jnp.log(jnp.sum(total, axis=1, keepdims=True))

    for r in (1, 3, 2):
        recv(p_z_in.at[(zh + r) % 4], z_sem.at[(zh + r) % 4])

    def finish(cp, carry):
        rows = pl.ds(pl.multiple_of(cp * 16, 16), 16)
        p = p_mine[cp]
        for r in (1, 3, 2):
            p = p + p_z_in[(zh + r) % 4, rows].astype(F32)
        lg = jnp.concatenate([logits[cp * 2], logits[cp * 2 + 1]], axis=0)
        term = p * (jnp.log(jnp.where(p > 0, p, 1.0)) - lg)
        mass, cross = carry
        return mass + p[0:8] + p[8:16], cross + term[0:8] + term[8:16]

    zero = jnp.zeros((8, 256), F32)
    mass, cross = unrolled(8, 4, finish, (zero, zero))
    mass = jnp.sum(mass, axis=1, keepdims=True)
    div = jnp.sum(cross, axis=1, keepdims=True) / mass - jnp.log(mass) + lse
    div_all[head] = jnp.broadcast_to(div, (8, 128))
    for dev in mates:
        send(div_all.at[head], div_all.at[head], div_sem.at[head], dev)

    for r in range(1, 8):
        d = (head + r) % 8
        recv(lg_all.at[d], lg_sem.at[d])
    for d in range(8):
        out_ref[8 * d:8 * d + 8, :] = lg_all[d]
    for copy in sends[:-7]:
        copy.wait_send()

    sent = [first_to_twin(dv) for dv in (1, 3, 2)]
    for du in range(4):
        sent += along_v(0, du) + (turn_along_z(0, du) if du < 2 else row_along_z(du) + along_v(1, du))
        sent += [turn_to_twin(0, 1, du)] + ([turn_to_twin(0, 0, du)] if du else [])
    for copy in sent:
        copy.wait_send()
    for r in range(1, 8):
        logits_copy(lax.rem(head + r, 8)).wait_send()

    for r in range(1, 8):
        d = (head + r) % 8
        recv(div_all.at[d], div_sem.at[d])
    column = jnp.concatenate([div_all[d] for d in range(8)] + [jnp.zeros((64, 128), F32)], axis=0)
    div_ref[...] = column.T[0:8]

    for copy in sends[-7:]:
        copy.wait_send()


def hand_over(logits_ref, div_ref, out_ref, out_div_ref):
    out_ref[...] = logits_ref[...]
    out_div_ref[...] = div_ref[0:1, 0:64]


def local(teacher_queries, latent_keys, index_queries, index_keys, index_weights, block_start):
    vmem = pl.BlockSpec(memory_space=pltpu.VMEM)
    dma = pltpu.SemaphoreType.DMA
    logits, div = pl.pallas_call(
        kernel,
        out_shape=(jax.ShapeDtypeStruct((64, 512), F32), jax.ShapeDtypeStruct((8, 128), F32)),
        in_specs=[
            pl.BlockSpec(memory_space=pl.ANY), vmem, vmem, vmem, vmem,
            pl.BlockSpec(memory_space=pltpu.SMEM),
        ],
        out_specs=(vmem, vmem),
        scratch_shapes=[
            pltpu.VMEM((64, 9216), BF16),
            pltpu.VMEM((1024, 640), BF16),
            pltpu.VMEM((2, 4, 4, 4, 16, 1408), BF16),
            pltpu.VMEM((2, 256, 640), BF16),
            pltpu.VMEM((2, 256, 128), BF16),
            pltpu.VMEM((2, 640, 256), BF16),
            pltpu.VMEM((2, 128, 256), BF16),
            pltpu.VMEM((8, 1024, 256), F32),
            pltpu.VMEM((16, 1024, 256), F32),
            pltpu.VMEM((8, 1024, 128), F32),
            pltpu.VMEM((8, 1024, 128), F32),
            pltpu.VMEM((8, 1024, 128), F32),
            pltpu.VMEM((8, 64, 128), BF16),
            pltpu.VMEM((512, 128), BF16),
            pltpu.VMEM((64, 128), F32),
            pltpu.VMEM((8, 8, 128), F32),
            pltpu.VMEM((512, 128), F32),
            pltpu.VMEM((16, 8, 256), F32),
            pltpu.VMEM((8, 8, 512), F32),
            pltpu.VMEM((8, 8, 512), F32),
            pltpu.VMEM((8, 16, 256), F32),
            pltpu.VMEM((4, 128, 256), BF16),
            pltpu.VMEM((4, 128, 256), BF16),
            pltpu.VMEM((4, 128, 256), BF16),
            pltpu.VMEM((4, 128, 256), BF16),
            pltpu.VMEM((8, 8, 128), F32),
            dma(()), dma((32,)),
            dma((8,)), dma((4,)), dma((8, 4)), dma((4, 2)), dma((2, 2)), dma((8,)),
            dma((2, 4, 3)), dma((2, 4)), dma((2, 4, 2)), dma((2, 4)),
            dma((8,)), dma((8,)), dma((8,)), dma((4,)), dma((4,)), dma((8,)),
        ],
        compiler_params=pltpu.CompilerParams(
            collective_id=0, has_side_effects=True, vmem_limit_bytes=56 << 20
        ),
    )(teacher_queries, latent_keys.T, index_queries, index_keys, index_weights.T, block_start)
    logits, div = pl.pallas_call(
        hand_over,
        out_shape=(jax.ShapeDtypeStruct((64, 512), F32), jax.ShapeDtypeStruct((1, 64), F32)),
        in_specs=[vmem, vmem],
        out_specs=(vmem, vmem),
    )(logits, div)
    return logits, div.reshape(64)


def solution(mesh):
    return jax.shard_map(
        local,
        mesh=mesh,
        in_specs=(
            P("ctx", "head"),
            P("ctx", None),
            P("ctx", "head"),
            P("ctx", None),
            P("ctx", "head"),
            P("ctx"),
        ),
        out_specs=(P("ctx", "head"), P("ctx")),
        check_vma=False,
    )
```

```python
import functools

import jax
import jax.numpy as jnp
from jax import lax
from jax.experimental import pallas as pl
from jax.experimental.pallas import tpu as pltpu
from jax.sharding import PartitionSpec as P

MESH = pl.DeviceIdType.MESH
F32, BF16 = jnp.float32, jnp.bfloat16
TEACHER_HEADS = 128
LATENT, ROPE, WIDTH, IDIM = 512, 64, 576, 128
NEG = -1e30
EXP_ROWS = 1024
EXP_SCALE = 192.0 ** (-0.5) * 1.4426950408889634
INDEX_SCALE = 128.0 ** (-0.5)
ORDER = (0, 1, 3, 2)


def unrolled(n, by, body, carry):
    def several(i, carry):
        for u in range(by):
            carry = body(i * by + u, carry)
        return carry

    return lax.fori_loop(0, n // by, several, carry)


def kernel(
    tq_hbm, lk_ref, iq_ref, ik_ref, iw_ref, bs_ref,
    out_ref, div_ref,
    tq, q_rows, keys, kc, ki, kct, kit, raw, expo, peaks, sums, wts,
    iq_send, iq_all, iw_send, iw_recv, iw_all, logits, lg_send, lg_all,
    p_mine, p_twin, p_twin_in, p_z, p_z_in, div_all,
    copy_sem, send_sem, twin_out, first_out, v_out, row_out, turn_out, lg_out, row_sem, col_sem, turn_sem, twin_in, iq_sem, iw_sem, lg_sem, twin_sem, z_sem, div_sem,
):
    ctx, head = lax.axis_index("ctx"), lax.axis_index("head")
    zl, x, y = ctx // 16, (ctx // 4) % 4, ctx % 4
    zh, core = head // 2, head % 2
    z = zh * 2 + zl
    pu, pv = x + core * (y - x), y + core * (x - y)
    twin = (ctx, zh * 2 + 1 - core)

    def ctx_of(par, u, v):
        u, v = lax.rem(u, 4), lax.rem(v, 4)
        return par * 16 + (u + core * (v - u)) * 4 + v + core * (u - v)

    def z_device(dz):
        zz = (z + dz + 8) % 8
        return ((zz % 2) * 16 + x * 4 + y, (zz // 2) * 2 + core)

    u_devs = {d: (ctx_of(zl, pu + d, pv), head) for d in (1, 3, 2)}
    v_devs = {d: (ctx_of(zl, pu, pv + d), head) for d in (1, 3, 2)}
    first_dev = z_device(2 * core - 1)
    last_dev = z_device(1 - 2 * core)
    mates = [(ctx, (head + r) % 8) for r in range(1, 8)]

    tq_copy = pltpu.make_async_copy(tq_hbm, tq, copy_sem)
    tq_copy.start()

    barrier = pltpu.get_barrier_semaphore()
    partners = list(u_devs.values()) + list(v_devs.values()) + [first_dev, last_dev] + mates
    for dev in partners:
        pl.semaphore_signal(barrier, inc=1, device_id=dev, device_id_type=MESH)

    lat = [lk_ref[128 * t:128 * t + 128, :].T for t in range(4)]
    rope = jnp.concatenate([lk_ref[512:576, :].astype(F32), jnp.zeros((64, 128), F32)], axis=0).T
    for g in range(4):
        a, b = g * 32, g * 32 + 16
        for t in range(4):
            keys[zl, x, y, g, :, 128 * t:128 * t + 128] = lat[t][a:a + 16]
            keys[zl, x, y, g, :, 640 + 128 * t:768 + 128 * t] = lat[t][b:b + 16]
        keys[zl, x, y, g, :, 512:640] = ik_ref[a:a + 16, :]
        keys[zl, x, y, g, :, 1152:1280] = ik_ref[b:b + 16, :]
        keys[zl, x, y, g, :, 1280:1408] = (rope[a:a + 16] + pltpu.roll(rope[b:b + 16], 64, 1)).astype(BF16)

    pl.semaphore_wait(barrier, len(partners))

    sends = []

    def remote(src, dst, out_sem, in_sem, dev):
        return pltpu.make_async_remote_copy(
            src_ref=src, dst_ref=dst, send_sem=out_sem, recv_sem=in_sem,
            device_id=dev, device_id_type=MESH,
        )

    def send(src, dst, in_sem, dev):
        copy = remote(src, dst, send_sem.at[len(sends)], in_sem, dev)
        copy.start()
        sends.append(copy)

    def recv(dst, in_sem):
        remote(dst, dst, send_sem.at[0], in_sem, twin).wait_recv()

    def copies(ref, out_sem, in_sem, dev):
        return remote(ref, ref, out_sem, in_sem, dev)

    def part(par, u, v, group=0, n=2):
        u, v = lax.rem(u, 4), lax.rem(v, 4)
        return keys.at[par, u + core * (v - u), v + core * (u - v), pl.ds(g0 + group, n)]

    def turn_part(which, par, u, group, n):
        u = lax.rem(u, 4)
        if which == 0:
            return keys.at[par, u, :, pl.ds(g0 + group, n)]
        return keys.at[par, :, u, pl.ds(g0 + group, n)]

    def by_core(start):
        for which in range(2):
            pl.when(core == which)(functools.partial(start, which))

    def along_v(par_rel, du):
        par = zl + par_rel * (1 - 2 * zl)
        return [
            copies(part(par, pu + du, pv), v_out.at[par_rel * 4 + du, dv],
                   col_sem.at[par, lax.rem(pu + du, 4)], v_devs[dv])
            for dv in (1, 3, 2)
        ]

    def row_along_z(du):
        return [
            copies(part(zl, pu + du, pv, g, 1), row_out.at[du, g],
                   row_sem.at[zl, lax.rem(pu + du, 4), 1 + g], dev)
            for g, dev in ((0, last_dev), (1, first_dev))
        ]

    def turn_along_z(which, du):
        return [
            copies(turn_part(which, zl, pu + du, g, 1), turn_out.at[du, g],
                   turn_sem.at[zl, lax.rem(pu + du, 4), g], dev)
            for g, dev in ((0, last_dev), (1, first_dev))
        ]

    def turn_to_twin(which, par_rel, du):
        par = zl + par_rel * (1 - 2 * zl)
        return copies(turn_part(which, par, pu + du, 0, 2), twin_out.at[par_rel * 4 + du],
                      twin_in.at[par, lax.rem(pu + du, 4)], twin)

    def first_to_twin(dv):
        return copies(part(zl, pu, pv + dv), first_out.at[dv], twin_in.at[zl, pu], twin)

    def start_all(several):
        for copy in several:
            copy.start()

    near = lambda devs: [devs[1], devs[3], devs[2]]
    g0 = 2 * core
    other = 1 - zl
    twin_half = 1 - core
    for dev in near(u_devs):
        send(part(zl, pu, pv), part(zl, pu, pv), row_sem.at[zl, pu, 0], dev)

    iqf = iq_ref[...].astype(F32)
    for d in range(8):
        iq_send[d] = jnp.concatenate(
            [iqf[8 * d:8 * d + 8, 128 * j:128 * j + 128] for j in range(8)], axis=0
        ).astype(BF16)
    weights = jnp.concatenate([iw_ref[...].astype(F32), jnp.zeros((8, 64), F32)], axis=1)
    weights = jnp.concatenate([weights, jnp.zeros((120, 128), F32)], axis=0).T
    iw_send[...] = weights[0:64]

    for r, dev in enumerate(mates):
        d = (head + r + 1) % 8
        send(iq_send.at[d], iq_all.at[pl.ds(pl.multiple_of(head * 64, 64), 64)], iq_sem.at[head], dev)
        send(iw_send.at[pl.ds(pl.multiple_of(d * 8, 8), 8)], iw_recv.at[head], iw_sem.at[head], dev)

    tq_copy.wait()
    lane = lax.broadcasted_iota(jnp.int32, (64, 128), 1)

    def prepare(i, carry):
        base = pl.multiple_of(i * 1152, 128)
        row = pl.multiple_of(i * 128, 128)
        q_rows[pl.ds(row, 64), 0:512] = tq[:, pl.ds(base, 512)]
        tiles = [tq[:, pl.ds(base + 512 + 128 * t, 128)].astype(F32) for t in range(5)]
        q_rows[pl.ds(row, 64), 512:640] = jnp.where(lane < 64, tiles[0], 0.0).astype(BF16)
        rolled = [pltpu.roll(t, 64, 1) for t in tiles]
        rolled.append(jnp.zeros_like(rolled[0]))
        for t in range(5):
            q_rows[pl.ds(row + 64, 64), 128 * t:128 * t + 128] = jnp.where(
                lane < 64, rolled[t], rolled[t + 1]
            ).astype(BF16)
        return carry

    start_all(along_v(0, 0))
    lax.fori_loop(0, 8, prepare, 0)

    for du in (1, 3, 2):
        recv(part(zl, pu + du, pv), row_sem.at[zl, lax.rem(pu + du, 4), 0])
        if du != 1:
            start_all(row_along_z(du))
        if du == 1:
            start_all(along_v(0, du))

    iq_all[pl.ds(pl.multiple_of(head * 64, 64), 64)] = iq_send[head]
    iw_recv[head] = iw_send[pl.ds(pl.multiple_of(head * 8, 8), 8)]
    for r in range(1, 8):
        d = (head + r) % 8
        recv(iq_all.at[pl.ds(pl.multiple_of(d * 64, 64), 64)], iq_sem.at[d])
        recv(iw_recv.at[d], iw_sem.at[d])
    for s in range(8):
        tile = iw_recv[s]
        for j in range(8):
            r = (s * 8 + j) * 8
            iw_all[r:r + 8, :] = jnp.broadcast_to(tile[:, j:j + 1], (8, 128))

    start0, start1 = bs_ref[0], bs_ref[1]

    def position(q):
        return jnp.where(q < 32, start0, start1) + q % 32

    def key_index(shape, par, half, w):
        sw, sj = 4 - 3 * half, 1 + 3 * half
        col = lax.broadcasted_iota(jnp.int32, shape, 1)
        return (par * 16 + w * sw) * 128 + half * 64 + (col // 64) * (sj * 128) + col % 64

    def assemble(slot, par, half, w):
        for j in range(4):
            kx, ky = w + half * (j - w), j + half * (w - j)
            for g in range(2):
                r = j * 64 + g * 32
                packed = keys[par, kx, ky, 2 * half + g]
                kc[slot, r:r + 16, 0:512] = packed[:, 0:512]
                ki[slot, r:r + 16, :] = packed[:, 512:640]
                kc[slot, r + 16:r + 32, 0:512] = packed[:, 640:1152]
                ki[slot, r + 16:r + 32, :] = packed[:, 1152:1280]
                rope = packed[:, 1280:1408]
                kc[slot, r:r + 16, 512:640] = rope
                kc[slot, r + 16:r + 32, 512:640] = pltpu.roll(rope.astype(F32), 64, 1).astype(BF16)
        kct[slot] = kc[slot].T
        kit[slot] = ki[slot].T

    def chunk(slot, held, par, half, w):
        ci = par * 8 + half * 4 + w
        shape = (64, 256)
        seen = key_index(shape, par, half, w) <= position(lax.broadcasted_iota(jnp.int32, shape, 0))
        bias = jnp.where(seen, 0.0, NEG)
        scores = jnp.dot(q_rows[...], kct[slot], preferred_element_type=F32)
        raw[held] = (scores.reshape(16, 64, 256) + bias[None]).reshape(1024, 256)

        s = jnp.dot(iq_all[...], kit[slot], preferred_element_type=F32)
        wt = iw_all[...]
        s = jnp.maximum(s, 0.0) * jnp.concatenate([wt, wt], axis=1)
        lg = jnp.sum(s.reshape(64, 8, 256), axis=0) * INDEX_SCALE
        shape = (8, 256)
        seen = key_index(shape, par, half, w) <= position(
            head * 8 + lax.broadcasted_iota(jnp.int32, shape, 0)
        )
        logits[ci] = jnp.where(seen, lg, 0.0)

    def pair_base(half):
        return x + half * (y - x)

    def exponentials(held, par, half, pair):
        base = pair_base(half)
        ca = par * 8 + half * 4 + lax.rem(base + 3 * pair, 4)
        cb = par * 8 + half * 4 + lax.rem(base + 1 + pair, 4)
        sc = (par * 2 + half) * 2 + pair
        held = held + 2 * half

        def block(rb, carry):
            rows = pl.ds(rb * EXP_ROWS, EXP_ROWS)
            refs = [(0, ca, 0), (0, ca, 128), (1, cb, 0), (1, cb, 128)]
            t = [raw[held + o, rows, l:l + 128] for o, _, l in refs]
            peak = jnp.maximum(jnp.maximum(t[0], t[1]), jnp.maximum(t[2], t[3]))
            e = [jnp.exp2((v - peak) * EXP_SCALE) for v in t]
            for (_, c, l), v in zip(refs, e):
                expo[c, rows, l:l + 128] = v
            peaks[sc, rows] = peak
            sums[sc, rows] = (e[0] + e[1]) + (e[2] + e[3])
            return carry

        block(0, 0)

    def logits_copy(j):
        return remote(lg_send.at[j], lg_all.at[head], lg_out.at[j], lg_sem.at[head], (ctx, j))

    def send_logits(par):
        for xx in range(4):
            j = par * 4 + xx
            for yy in range(4):
                a = logits[par * 8 + xx, :, 64 * yy:64 * yy + 64]
                b = logits[par * 8 + 4 + yy, :, 64 * xx:64 * xx + 64]
                lg_send[j, :, 128 * yy:128 * yy + 128] = jnp.concatenate([a, b], axis=1)

            @pl.when(j != head)
            def _():
                logits_copy(j).start()

            @pl.when(j == head)
            def _():
                lg_all[head] = lg_send[j]

    def turn_of(i):
        par_rel = jnp.where((i == 2) | (i >= 5), 1, 0)
        du = jnp.where(i < 2, i, jnp.where(i < 5, lax.rem(6 - i, 4), jnp.where(i == 5, 1, 9 - i)))
        return par_rel, du, zl + par_rel * (1 - 2 * zl)

    def recv_col(par, du):
        recv(keys.at[par, 0, pl.ds(0, 3), pl.ds(0, 2)], col_sem.at[par, lax.rem(pu + du, 4)])

    def arrivals(par_rel, du):
        @pl.when(par_rel == 0)
        def _():
            recv_col(zl, du)
            pl.when(du == 1)(lambda: by_core(lambda which: start_all(turn_along_z(which, 1))))

        @pl.when((par_rel == 1) & (du < 2))
        def _():
            for g in range(2):
                recv(keys.at[other, 0, :, pl.ds(0, 1)], turn_sem.at[other, lax.rem(pu + du, 4), g])

        @pl.when((par_rel == 1) & (du >= 2))
        def _():
            recv_col(other, du)

        by_core(lambda which: turn_to_twin(which, par_rel, du).start())

    def step(i, carry):
        par_rel, du, par = turn_of(i)
        pair = lax.div(du, 2)
        second = jnp.where(pair == 1, 3 - du, du)
        w_mine = lax.rem(pair_base(core) + du, 4)
        w_twin = lax.rem(pair_base(twin_half) + du, 4)

        held = par_rel * 4 + second
        next_rel, next_du, _ = turn_of(i + 1)

        @pl.when(i == 0)
        def _():
            recv(keys.at[par, 0, pl.ds(0, 3), pl.ds(0, 2)], twin_in.at[par, w_twin])

        @pl.when(i > 0)
        def _():
            recv(keys.at[par, 0, :, pl.ds(0, 2)], twin_in.at[par, w_twin])

        @pl.when((i >= 1) & (i < 7))
        def _():
            arrivals(next_rel, next_du)

        @pl.when(i == 0)
        def _():
            start_all(along_v(0, 3))

        assemble(0, par, core, w_mine)
        assemble(1, par, twin_half, w_twin)
        chunk(0, held + 2 * core, par, core, w_mine)
        chunk(1, held + 2 * twin_half, par, twin_half, w_twin)

        @pl.when(i == 0)
        def _():
            start_all(along_v(0, 2))
            for eu in (3, 2):
                for g in range(2):
                    recv(part(other, pu + eu, pv, g, 1), row_sem.at[other, lax.rem(pu + eu, 4), 1 + g])
                start_all(along_v(1, eu))

        @pl.when(i < 1)
        def _():
            arrivals(next_rel, next_du)

        @pl.when((i == 1) | (i == 4) | (i == 5) | (i == 7))
        def _():
            exponentials(par_rel * 4, par, 0, pair)
            exponentials(par_rel * 4, par, 1, pair)

        @pl.when((i == 4) | (i == 7))
        def _():
            send_logits(par)

        return carry

    recv_col(zl, 0)
    by_core(lambda which: start_all(turn_along_z(which, 0)))
    for dv in (1, 3, 2):
        first_to_twin(dv).start()
    lax.fori_loop(0, 8, step, 0)

    def normalise(rb, carry):
        rows = pl.ds(pl.multiple_of(rb * 512, 512), 512)
        m = [peaks[s, rows] for s in range(8)]
        top = jnp.max(functools.reduce(jnp.maximum, m), axis=1, keepdims=True)
        w = [jnp.exp2((v - top) * EXP_SCALE) for v in m]
        total = functools.reduce(jnp.add, [sums[s, rows] * w[s] for s in range(8)])
        share = 1.0 / (jnp.sum(total, axis=1, keepdims=True) * TEACHER_HEADS)
        for s in range(8):
            wts[s, rows] = w[s] * share
        return carry

    lax.fori_loop(0, 2, normalise, 0)

    def weigh(cp, d):
        parts = []
        for o in range(2):
            ci = cp * 2 + o
            sch = ci // 4
            half = sch % 2
            sc = sch * 2 + ((ci % 4 - pair_base(half) + 4) % 4) // 2
            acc = None
            for j in range(16):
                rows = pl.ds(pl.multiple_of(j * 64 + d * 8, 8), 8)
                wt = wts[sc, rows]
                term = expo[ci, rows] * jnp.concatenate([wt, wt], axis=1)
                acc = term if acc is None else acc + term
            parts.append(acc)
        return jnp.concatenate(parts, axis=0)

    for r in (2, 1, 3, 0):
        zi = (zh + r) % 4

        def to_twin(cp, carry):
            p_twin[zi, pl.ds(pl.multiple_of(cp * 16, 16), 16)] = weigh(cp, zi * 2 + 1 - core).astype(BF16)
            return carry

        unrolled(8, 8, to_twin, 0)
        send(p_twin.at[zi], p_twin_in.at[zi], twin_sem.at[zi], twin)

    for r in (2, 1, 3, 0):
        zi = (zh + r) % 4

        recv(p_twin_in.at[zi], twin_sem.at[zi])

        def mine(cp, carry):
            rows = pl.ds(pl.multiple_of(cp * 16, 16), 16)
            p = weigh(cp, zi * 2 + core) + p_twin_in[zi, rows].astype(F32)
            if r:
                p_z[zi, rows] = p.astype(BF16)
            else:
                p_mine[cp] = p
            return carry

        unrolled(8, 8, mine, 0)
        if r:
            send(p_z.at[zi], p_z_in.at[zh], z_sem.at[zh], (ctx, zi * 2 + core))

    shape = (8, 256)
    pos8 = position(head * 8 + lax.broadcasted_iota(jnp.int32, shape, 0))
    masked = []
    for ci in range(16):
        seen = key_index(shape, ci // 8, (ci // 4) % 2, ci % 4) <= pos8
        masked.append(jnp.where(seen, logits[ci], NEG))
    top = jnp.max(functools.reduce(jnp.maximum, masked), axis=1, keepdims=True)
    total = functools.reduce(jnp.add, [jnp.exp(v - top) for v in masked])
    lse = top + jnp.log(jnp.sum(total, axis=1, keepdims=True))

    for r in (1, 3, 2):
        recv(p_z_in.at[(zh + r) % 4], z_sem.at[(zh + r) % 4])

    def finish(cp, carry):
        rows = pl.ds(pl.multiple_of(cp * 16, 16), 16)
        p = p_mine[cp]
        for r in (1, 3, 2):
            p = p + p_z_in[(zh + r) % 4, rows].astype(F32)
        lg = jnp.concatenate([logits[cp * 2], logits[cp * 2 + 1]], axis=0)
        term = p * (jnp.log(jnp.where(p > 0, p, 1.0)) - lg)
        mass, cross = carry
        return mass + p[0:8] + p[8:16], cross + term[0:8] + term[8:16]

    zero = jnp.zeros((8, 256), F32)
    mass, cross = unrolled(8, 4, finish, (zero, zero))
    mass = jnp.sum(mass, axis=1, keepdims=True)
    div = jnp.sum(cross, axis=1, keepdims=True) / mass - jnp.log(mass) + lse
    div_all[head] = jnp.broadcast_to(div, (8, 128))
    for dev in mates:
        send(div_all.at[head], div_all.at[head], div_sem.at[head], dev)

    for r in range(1, 8):
        d = (head + r) % 8
        recv(lg_all.at[d], lg_sem.at[d])
    for d in range(8):
        out_ref[8 * d:8 * d + 8, :] = lg_all[d]
    for copy in sends[:-7]:
        copy.wait_send()

    sent = [first_to_twin(dv) for dv in (1, 3, 2)]
    for du in range(4):
        sent += along_v(0, du) + (turn_along_z(0, du) if du < 2 else row_along_z(du) + along_v(1, du))
        sent += [turn_to_twin(0, 1, du)] + ([turn_to_twin(0, 0, du)] if du else [])
    for copy in sent:
        copy.wait_send()
    for r in range(1, 8):
        logits_copy(lax.rem(head + r, 8)).wait_send()

    for r in range(1, 8):
        d = (head + r) % 8
        recv(div_all.at[d], div_sem.at[d])
    column = jnp.concatenate([div_all[d] for d in range(8)] + [jnp.zeros((64, 128), F32)], axis=0)
    div_ref[...] = column.T[0:8]

    for copy in sends[-7:]:
        copy.wait_send()


def hand_over(logits_ref, div_ref, out_ref, out_div_ref):
    out_ref[...] = logits_ref[...]
    out_div_ref[...] = div_ref[0:1, 0:64]


def local(teacher_queries, latent_keys, index_queries, index_keys, index_weights, block_start):
    vmem = pl.BlockSpec(memory_space=pltpu.VMEM)
    dma = pltpu.SemaphoreType.DMA
    logits, div = pl.pallas_call(
        kernel,
        out_shape=(jax.ShapeDtypeStruct((64, 512), F32), jax.ShapeDtypeStruct((8, 128), F32)),
        in_specs=[
            pl.BlockSpec(memory_space=pl.ANY), vmem, vmem, vmem, vmem,
            pl.BlockSpec(memory_space=pltpu.SMEM),
        ],
        out_specs=(vmem, vmem),
        scratch_shapes=[
            pltpu.VMEM((64, 9216), BF16),
            pltpu.VMEM((1024, 640), BF16),
            pltpu.VMEM((2, 4, 4, 4, 16, 1408), BF16),
            pltpu.VMEM((2, 256, 640), BF16),
            pltpu.VMEM((2, 256, 128), BF16),
            pltpu.VMEM((2, 640, 256), BF16),
            pltpu.VMEM((2, 128, 256), BF16),
            pltpu.VMEM((8, 1024, 256), F32),
            pltpu.VMEM((16, 1024, 256), F32),
            pltpu.VMEM((8, 1024, 128), F32),
            pltpu.VMEM((8, 1024, 128), F32),
            pltpu.VMEM((8, 1024, 128), F32),
            pltpu.VMEM((8, 64, 128), BF16),
            pltpu.VMEM((512, 128), BF16),
            pltpu.VMEM((64, 128), F32),
            pltpu.VMEM((8, 8, 128), F32),
            pltpu.VMEM((512, 128), F32),
            pltpu.VMEM((16, 8, 256), F32),
            pltpu.VMEM((8, 8, 512), F32),
            pltpu.VMEM((8, 8, 512), F32),
            pltpu.VMEM((8, 16, 256), F32),
            pltpu.VMEM((4, 128, 256), BF16),
            pltpu.VMEM((4, 128, 256), BF16),
            pltpu.VMEM((4, 128, 256), BF16),
            pltpu.VMEM((4, 128, 256), BF16),
            pltpu.VMEM((8, 8, 128), F32),
            dma(()), dma((32,)),
            dma((8,)), dma((4,)), dma((8, 4)), dma((4, 2)), dma((2, 2)), dma((8,)),
            dma((2, 4, 3)), dma((2, 4)), dma((2, 4, 2)), dma((2, 4)),
            dma((8,)), dma((8,)), dma((8,)), dma((4,)), dma((4,)), dma((8,)),
        ],
        compiler_params=pltpu.CompilerParams(
            collective_id=0, has_side_effects=True, vmem_limit_bytes=56 << 20
        ),
    )(teacher_queries, latent_keys.T, index_queries, index_keys, index_weights.T, block_start)
    logits, div = pl.pallas_call(
        hand_over,
        out_shape=(jax.ShapeDtypeStruct((64, 512), F32), jax.ShapeDtypeStruct((1, 64), F32)),
        in_specs=[vmem, vmem],
        out_specs=(vmem, vmem),
    )(logits, div)
    return logits, div.reshape(64)


def solution(mesh):
    return jax.shard_map(
        local,
        mesh=mesh,
        in_specs=(
            P("ctx", "head"),
            P("ctx", None),
            P("ctx", "head"),
            P("ctx", None),
            P("ctx", "head"),
            P("ctx"),
        ),
        out_specs=(P("ctx", "head"), P("ctx")),
        check_vma=False,
    )
```
